32 devices in a mesh: seq: 16 (over z, y, core), mp: 2 (over x).
Axes of the slice: x: 2, y: 2, z: 4, core: 2. Of those that a mesh axis runs over, the one named last changes fastest.
Arguments:
- patches: bfloat16 [4096, 64], P('seq'), may hold values from -6 to 6
- clip_shape: int32 [8, 3], replicated, may hold values from 1 to 16, as said below
- shard_counts: int32 [16], replicated, may hold values from 1 to 256, as said below
- patch_weight: bfloat16 [64, 2560], P(None, 'mp'), may hold values from -3 to 3
- patch_bias: float32 [2560], P('mp'), may hold values from -6 to 6
- time_mod: float32 [8, 2, 2560], P(None, None, 'mp'), may hold values from -6 to 6
- block_mod: float32 [2, 2560], P(None, 'mp'), may hold values from -4 to 4
- w_query: bfloat16 [2560, 2560], P('seq', 'mp'), may hold values from -0.47434165 to 0.47434165
- query_bias: float32 [2560], P('mp'), may hold values from -4 to 4
- w_keyvalue: bfloat16 [2560, 5120], P('seq', 'mp'), may hold values from -0.47434165 to 0.47434165
- keyvalue_bias: float32 [5120], P('mp'), may hold values from -6 to 6
- norm_gain: float32 [2, 2560], P(None, 'mp'), may hold values from 1 to 2
Outputs:
- attention: bfloat16 [4096, 2560], P('seq', 'mp')
The draws below stay inside these ranges and needn't reach their ends.
Inputs may be any that keep to these rules, and one draw needn't show every extreme that they name: `clip_shape`: clip c lies on shards 2 c to 2 c + 1. Frames run from 1 to 2, patch rows from 8 to 16, patch columns from 8 to 16; some clip has 2 frames of 16 by 16 patches. `shard_counts`: the counts of clip c's 2 shards add up to the product of clip_shape[c].
All inputs are finite; a program needn't handle non-finite values.
Results may differ from the reference program's by a relative error of at most 0.0063.
Values may be sent and summed in bfloat16 or wider, within the bound.
No kernel may reach another device: no remote copies, remote signals or barrier semaphores. Data moves between devices by JAX's collectives and lax.ppermute only.
A program may use at most 128 MiB of HBM per device.

```python
import math
import jax
import jax.numpy as jnp
from jax import lax

D = 2560
HEADS = 20
HD = 128
CIN = 64
GROUP = 2
TOK_DEV = 256
CLIPS = 8
SLOTS = 4096


def clip_layout(key):
    base_key = jax.random.fold_in(key, 71)
    key_frames, key_height, key_width, key_pick, key_split, key_order = jax.random.split(base_key, 6)
    frames = jax.random.randint(key_frames, (CLIPS,), 1, 3)
    height = jax.random.randint(key_height, (CLIPS,), 8, 17)
    widths = jax.random.randint(key_width, (CLIPS,), TOK_DEV // 32, TOK_DEV // 16 + 1)
    chosen = jax.random.randint(key_pick, (), 0, CLIPS)
    smallest = (chosen + 1) % CLIPS
    clip_ids = jnp.arange(CLIPS)
    frames = jnp.where(clip_ids == chosen, 2, jnp.where(clip_ids == smallest, 1, frames))
    height = jnp.where(clip_ids == chosen, 16, jnp.where(clip_ids == smallest, 8, height))
    widths = jnp.where(clip_ids == chosen, TOK_DEV // 16, jnp.where(clip_ids == smallest, TOK_DEV // 32, widths))
    sizes = frames * height * widths
    share = sizes // GROUP
    spare = sizes % GROUP
    margin = jnp.maximum(jnp.minimum(TOK_DEV - share - 1, share - 1), 0)
    shifts = jax.random.randint(key_split, (CLIPS, GROUP // 2), -margin[:, None], margin[:, None] + 1)
    parts = share[:, None] + jnp.concatenate([shifts, -shifts], axis=1)
    parts = parts + jnp.where(jnp.arange(GROUP)[None, :] < spare[:, None], 1, 0)
    order_keys = jax.random.split(key_order, CLIPS)
    parts = jax.vmap(lambda one_key, one_row: jax.random.permutation(one_key, one_row))(order_keys, parts)
    shapes = jnp.stack([frames, height, widths], axis=1).astype(jnp.int32)
    return (shapes, parts.reshape(CLIPS * GROUP).astype(jnp.int32))


def draw_clip_shape(key, part):
    return clip_layout(key)[0]


def draw_shard_counts(key, part):
    return clip_layout(key)[1]


def base_values(key, rows, columns):
    return (jnp.clip(jax.random.normal(key, (rows, columns), jnp.float32), -4.0, 4.0), 3.0)


def draw_patch_weight(key, part):
    key_base, key_scale = jax.random.split(jax.random.fold_in(key, 13))
    values, ramp_base = base_values(key_base, CIN, D)
    rising = ramp_base ** (jnp.arange(D, dtype=jnp.float32) / (D - 1))
    column = jnp.exp(jax.random.uniform(key_scale, (D,), jnp.float32, math.log(0.5), math.log(2.0)))
    return (values * column[None, :] * rising[None, :] / math.sqrt(CIN)).astype(jnp.bfloat16)


def projection_values(key, columns, head_width, ramped):
    key_base, key_scale = jax.random.split(key)
    values, ramp_base = base_values(key_base, D, columns)
    column_ids = jnp.arange(columns)
    head_ids = (column_ids // head_width).astype(jnp.float32)
    rising = jnp.where(ramped(column_ids), ramp_base ** (head_ids / (HEADS - 1)), 1.0)
    column = jnp.exp(jax.random.uniform(key_scale, (columns,), jnp.float32, math.log(0.5), math.log(2.0)))
    return (values * column[None, :] * rising[None, :] / math.sqrt(D)).astype(jnp.bfloat16)


def draw_w_query(key, part):
    return projection_values(jax.random.fold_in(key, 29), HEADS * HD, HD, lambda column_ids: column_ids >= 0)


def draw_w_keyvalue(key, part):
    return projection_values(jax.random.fold_in(key, 37), HEADS * 2 * HD, 2 * HD, lambda column_ids: column_ids // HD % 2 == 0)


def shard_levels(own_key, dims, shards, low, top_value):
    def one(dim, blocks):
        steps = jax.random.uniform(jax.random.fold_in(jax.random.fold_in(own_key, 6), dim), (blocks,), jnp.float32, low / len(shards), top_value / len(shards))
        return jnp.repeat(jnp.exp(steps), dims[dim] // blocks).reshape((-1,) + (1,) * (len(dims) - dim - 1))

    loudness = one(*shards[0])
    for cut in shards[1:]:
        loudness = loudness * one(*cut)
    return loudness


def normal_values(own_key, dims, scale, limit, pieces=(), kind=jnp.bfloat16):
    drawn = scale * jax.random.normal(own_key, dims, jnp.float32)
    if pieces:
        drawn = drawn * shard_levels(own_key, dims, pieces, -0.22, 0.18)
    return jnp.clip(drawn, -limit, limit).astype(kind)


def setup_inputs(seed: int = 0) -> dict:
    seeds = jax.random.split(jax.random.key(seed), 13)
    patches = normal_values(seeds[0], (SLOTS, CIN), 1.0, 6.0, ((0, 16),))
    clip_shape = draw_clip_shape(jax.random.fold_in(seeds[12], 71), 0)
    shard_counts = draw_shard_counts(jax.random.fold_in(seeds[12], 71), 0)
    patch_weight = draw_patch_weight(jax.random.fold_in(seeds[12], 71), 0)
    patch_bias = normal_values(seeds[4], (D,), 1.0, 6.0, ((0, 2),), jnp.float32)
    time_mod = normal_values(seeds[5], (CLIPS, 2, D), 0.5, 6.0, ((2, 2),), jnp.float32)
    block_mod = normal_values(seeds[6], (2, D), 0.3, 4.0, ((1, 2),), jnp.float32)
    w_query = draw_w_query(jax.random.fold_in(seeds[12], 71), 0)
    query_bias = normal_values(seeds[8], (HEADS * HD,), 0.3, 4.0, ((0, 2),), jnp.float32)
    w_keyvalue = draw_w_keyvalue(jax.random.fold_in(seeds[12], 71), 0)
    keyvalue_bias = normal_values(seeds[10], (HEADS * 2 * HD,), 0.5, 6.0, ((0, 2),), jnp.float32)
    norm_gain = jnp.clip(jnp.exp(math.log(2.0) - 0.6931472 * jax.random.uniform(seeds[11], (2, HEADS * HD), jnp.float32) ** shard_levels(seeds[11], (2, HEADS * HD), ((1, 2),), -0.2, 0.2)), 1.0, 2.0)
    return dict(patches=patches, clip_shape=clip_shape, shard_counts=shard_counts, patch_weight=patch_weight, patch_bias=patch_bias, time_mod=time_mod, block_mod=block_mod, w_query=w_query, query_bias=query_bias, w_keyvalue=w_keyvalue, keyvalue_bias=keyvalue_bias, norm_gain=norm_gain)


EPSILON = 1e-06

def rounded(values):
    return lax.optimization_barrier(values.astype(jnp.bfloat16)).astype(jnp.float32)

def token_places(group_counts, member_ids, slot_ids, shape_row):
    before = (jnp.cumsum(group_counts) - group_counts).astype(jnp.int32)
    lookup = jnp.arange(GROUP, dtype=jnp.int32)[None, :] == member_ids[:, None]
    offset = lax.optimization_barrier(jnp.sum(jnp.where(lookup, before[None, :], 0), axis=1)).astype(jnp.int32)
    holding = lax.optimization_barrier(jnp.sum(jnp.where(lookup, group_counts[None, :], 0), axis=1)).astype(jnp.int32)
    position = offset + slot_ids
    plane_size = shape_row[1] * shape_row[2]
    frame_pos = position // plane_size
    row_pos = position // shape_row[2] % shape_row[1]
    col_pos = position % shape_row[2]
    return (slot_ids < holding, frame_pos, row_pos, col_pos)

def rotary_tables(frame_pos, row_pos, col_pos):
    other_pairs = HD // 6
    frame_pairs = HD // 2 - 2 * other_pairs
    pair_id = jnp.arange(HD, dtype=jnp.int32) // 2
    in_frame = pair_id < frame_pairs
    in_row = jnp.logical_and(pair_id >= frame_pairs, pair_id < frame_pairs + other_pairs)
    within = jnp.where(in_frame, pair_id, jnp.where(in_row, pair_id - frame_pairs, pair_id - frame_pairs - other_pairs)).astype(jnp.float32)
    axis_span = jnp.where(in_frame, 2.0 * frame_pairs, 2.0 * other_pairs).astype(jnp.float32)
    inverse = jnp.exp(-(2.0 * within / axis_span) * math.log(10000.0))
    position = jnp.where(in_frame[None, :], frame_pos[:, None], jnp.where(in_row[None, :], row_pos[:, None], col_pos[:, None])).astype(jnp.float32)
    angles = position * inverse[None, :]
    return (jnp.cos(angles), jnp.sin(angles))

def rotate_pairs(values, cosine_table, sine_table):
    parity = jnp.arange(HD, dtype=jnp.int32) % 2 == 0
    partner = jnp.where(parity, -jnp.roll(values, -1, axis=-1), jnp.roll(values, 1, axis=-1))
    return values * cosine_table[:, None, :] + partner * sine_table[:, None, :]

def modulate_rows(embedded, row_sums, squares, modulation):
    average = row_sums / D
    variance = squares / D - average * average
    normed = (embedded - average[:, None]) * lax.rsqrt(variance[:, None] + EPSILON)
    return (normed * (1.0 + modulation[1]) + modulation[0]).astype(jnp.bfloat16)

def finish_heads(raw_rows, squares, scale_gain, cosine_table, sine_table):
    normed = raw_rows * lax.rsqrt(squares[:, None] / (HEADS * HD) + EPSILON) * scale_gain
    return rotate_pairs(normed.reshape(raw_rows.shape[0], -1, HD), cosine_table, sine_table).astype(jnp.bfloat16)

def reference(patches, clip_shape, shard_counts, patch_weight, patch_bias, time_mod, block_mod, w_query, query_bias, w_keyvalue, keyvalue_bias, norm_gain):
    span_rows = GROUP * TOK_DEV
    highest = lax.Precision.HIGHEST

    def one_clip(clip_id):
        row_block = lax.dynamic_slice_in_dim(patches, (clip_id * span_rows).astype(jnp.int32), span_rows, 0)
        group_counts = lax.dynamic_slice_in_dim(shard_counts, (clip_id * GROUP).astype(jnp.int32), GROUP, 0)
        shape_row = lax.dynamic_index_in_dim(clip_shape, clip_id, 0, keepdims=False)
        slot_all = jnp.arange(span_rows, dtype=jnp.int32)
        is_valid, frame_pos, row_pos, col_pos = token_places(group_counts, slot_all // TOK_DEV, slot_all % TOK_DEV, shape_row)
        modulation = lax.dynamic_index_in_dim(time_mod, clip_id, 0, keepdims=False) + block_mod
        embedded = jnp.dot(row_block, patch_weight, preferred_element_type=jnp.float32) + patch_bias
        hidden = modulate_rows(embedded, lax.optimization_barrier(jnp.sum(embedded, axis=1)), lax.optimization_barrier(jnp.sum(embedded * embedded, axis=1)), modulation)
        query_raw = jnp.dot(hidden, w_query, preferred_element_type=jnp.float32) + query_bias
        pair_raw = (jnp.dot(hidden, w_keyvalue, preferred_element_type=jnp.float32) + keyvalue_bias).reshape(span_rows, HEADS, 2, HD)
        key_raw = pair_raw[:, :, 0].reshape(span_rows, HEADS * HD)
        value_rows = rounded(pair_raw[:, :, 1])
        cosine_table, sine_table = rotary_tables(frame_pos, row_pos, col_pos)
        queries = finish_heads(query_raw, lax.optimization_barrier(jnp.sum(query_raw * query_raw, axis=1)), norm_gain[0], cosine_table, sine_table)
        key_rows = finish_heads(key_raw, lax.optimization_barrier(jnp.sum(key_raw * key_raw, axis=1)), norm_gain[1], cosine_table, sine_table)
        queries = lax.optimization_barrier(queries).astype(jnp.float32)
        key_rows = lax.optimization_barrier(key_rows).astype(jnp.float32)
        scores = jnp.einsum('qhd,khd->hqk', queries, key_rows, precision=highest) * HD ** (-0.5)
        weights = jnp.where(is_valid[None, None, :], jnp.exp(scores), 0.0)
        totals = lax.optimization_barrier(jnp.sum(weights, axis=-1))
        numerator = jnp.einsum('hqk,khd->qhd', rounded(weights), value_rows, precision=highest)
        result = numerator / jnp.transpose(totals)[:, :, None]
        result = jnp.where(is_valid[:, None, None], result, 0.0)
        return result.reshape(span_rows, HEADS * HD).astype(jnp.bfloat16)
    outputs = lax.map(one_clip, jnp.arange(CLIPS, dtype=jnp.int32))
    return outputs.reshape(SLOTS, HEADS * HD)
```

```python
import functools
import math

import jax
import jax.numpy as jnp
from jax import lax
from jax.experimental import pallas as pl
from jax.experimental.pallas import tpu as pltpu
from jax.sharding import PartitionSpec as P

D = 2560
HEADS = 20
HD = 128
GROUP = 2
EPSILON = 1e-06

BLOCKS = 4
WIRE = 72
STEP = 80
VMEM_LIMIT = 48 * 1024 * 1024
F32 = jnp.float32
BF16 = jnp.bfloat16


def params():
    return pltpu.CompilerParams(vmem_limit_bytes=VMEM_LIMIT)


def vmem():
    return pl.BlockSpec(memory_space=pltpu.VMEM)


def smem():
    return pl.BlockSpec(memory_space=pltpu.SMEM)


def swap_bits(value, mask):
    count = lax.axis_size("seq")
    return lax.ppermute(value, "seq", [(source, source ^ mask) for source in range(count)])


def exact_pieces(values, pieces):
    found = []
    for _ in range(pieces):
        piece = values.astype(BF16)
        found.append(piece)
        values = values - piece.astype(F32)
    return found


def chip_block():
    return lax.rem(lax.div(lax.axis_index("seq"), 2), BLOCKS)


def pack_kernel(wq_ref, wkv_ref, *out_refs):
    mine = chip_block()
    wide = out_refs[0].shape[1]
    query_cols, pair_cols = wq_ref.shape[1], wkv_ref.shape[1]
    for flip in range(BLOCKS):
        for block in range(BLOCKS):

            @pl.when(jnp.bitwise_xor(mine, flip) == block)
            def _(flip=flip, block=block):
                first, last = block * wide, (block + 1) * wide
                spans = [
                    (wq_ref, 0, query_cols),
                    (wkv_ref, query_cols, query_cols + pair_cols),
                    (None, query_cols + pair_cols, BLOCKS * wide),
                ]
                for ref, low, high in spans:
                    start, stop = max(first, low), min(last, high)
                    if start >= stop:
                        continue
                    here = pl.ds(start - first, stop - start)
                    if ref is None:
                        out_refs[flip][:, here] = jnp.zeros((wq_ref.shape[0], stop - start), BF16)
                    else:
                        out_refs[flip][:, here] = ref[:, pl.ds(start - low, stop - start)]


def pack_weights(w_query, w_keyvalue):
    rows = w_query.shape[0]
    wide = -(-(w_query.shape[1] + w_keyvalue.shape[1]) // (BLOCKS * HD)) * HD
    return pl.pallas_call(
        pack_kernel,
        out_shape=[jax.ShapeDtypeStruct((rows, wide), BF16)] * BLOCKS,
        in_specs=[vmem()] * 2,
        out_specs=[vmem()] * BLOCKS,
        compiler_params=params(),
        name="pack_weights",
    )(w_query, w_keyvalue)


def modulated_kernel(clips_sent, whole_ref, part_ref, mods_ref, high_ref, low_ref):
    place = lax.axis_index("seq")
    rest, core = lax.div(place, 4), lax.rem(place, 2)
    total = jnp.zeros((72, 1), F32)
    for shard in range(whole_ref.shape[0]):
        total = total + jnp.sum(whole_ref[shard, 0:72], axis=1, keepdims=True)
    centred = part_ref[...] - total * (1.0 / D)
    row = lax.broadcasted_iota(jnp.int32, (STEP - 64, centred.shape[1]), 0)
    for flip in range(clips_sent):
        clip = jnp.bitwise_xor(rest, flip) * 2 + core
        mods = mods_ref[clip]
        shift, scale = mods[0:1], 1.0 + mods[1:2]
        patch_rows = centred[0:64] * scale
        extra = jnp.where(row == 0, centred[64:65] * scale, jnp.where(row == 1, shift, 0.0))
        for start, values in ((0, patch_rows), (64, extra)):
            high, low = exact_pieces(values, 2)
            here = pl.ds(flip * STEP + start, values.shape[0])
            high_ref[here] = high
            low_ref[here] = low


def modulated_rows(whole, part, mods, clips_sent):
    shape = jax.ShapeDtypeStruct((clips_sent * STEP, part.shape[1]), BF16)
    return pl.pallas_call(
        functools.partial(modulated_kernel, clips_sent),
        out_shape=[shape, shape],
        in_specs=[vmem()] * 3,
        out_specs=[vmem()] * 2,
        compiler_params=params(),
        name="modulated_rows",
    )(whole, part, mods)


def product_kernel(clips_sent, *refs):
    high_ref, low_ref = refs[:2]
    piece_refs = refs[2 : 2 + 2 * BLOCKS]
    out_refs = refs[2 + 2 * BLOCKS : 2 + 2 * BLOCKS + clips_sent]
    weight, sems = refs[2 + 2 * BLOCKS + clips_sent :]
    rows = piece_refs[0].shape[0]
    core = lax.rem(lax.axis_index("seq"), 2)
    mine = chip_block()
    copies = []
    for order in range(2 * BLOCKS):
        flip, other = order // 2, order % 2
        source = jnp.bitwise_xor(mine, flip) * 2 + jnp.bitwise_xor(core, other)
        here = pl.ds(pl.multiple_of(source * rows, 16), rows)
        copies.append(
            pltpu.make_async_copy(piece_refs[order], weight.at[here], sems.at[order])
        )
    for copy in copies:
        copy.start()
    for copy in copies:
        copy.wait()
    wide = weight.shape[1]
    tile = 256
    for start in range(0, wide, tile):
        columns = pl.ds(start, tile)
        block = weight[:, columns]
        total = jnp.dot(high_ref[...], block, preferred_element_type=F32)
        total = total + jnp.dot(low_ref[...], block, preferred_element_type=F32)
        for flip in range(clips_sent):
            base = flip * STEP
            ends = total[base + 64 : base + 72]
            first = ends.astype(BF16).astype(F32)
            ends = first + pltpu.roll(ends - first, 2, 0)
            out_refs[flip][:, columns] = jnp.concatenate(
                [total[base : base + 64], ends], axis=0
            ).astype(BF16)


def product_rows(high, low, pieces, clips_sent):
    rows, wide = pieces[0].shape
    return pl.pallas_call(
        functools.partial(product_kernel, clips_sent),
        out_shape=[jax.ShapeDtypeStruct((WIRE, wide), BF16)] * clips_sent,
        in_specs=[vmem()] * 2 + [pl.BlockSpec(memory_space=pl.ANY)] * len(pieces),
        out_specs=[vmem()] * clips_sent,
        scratch_shapes=[
            pltpu.VMEM((2 * BLOCKS * rows, wide), BF16),
            pltpu.SemaphoreType.DMA((2 * BLOCKS,)),
        ],
        compiler_params=params(),
        name="product_rows",
    )(high, low, *pieces)


def split_ends(ends, row):
    ends = jnp.where(row < 2, ends + pltpu.roll(ends, 6, 0), 0.0)
    first = ends.astype(BF16).astype(F32)
    return first + pltpu.roll(ends - first, 2, 0)


def sum_kernel(*refs):
    in_refs, out_ref = refs[:-1], refs[-1]
    own = lax.rem(lax.div(lax.axis_index("seq"), 4), 2)
    row = lax.broadcasted_iota(jnp.int32, (8, out_ref.shape[2]), 0)
    for parity in range(2):
        total = in_refs[parity][...].astype(F32)
        for ref in in_refs[parity + 2 :: 2]:
            total = total + ref[...].astype(F32)
        ends = split_ends(total[64:72], row)
        out_ref[jnp.bitwise_xor(own, parity)] = jnp.concatenate([total[0:64], ends], axis=0).astype(
            BF16
        )


def sum_rows(arrived):
    return pl.pallas_call(
        sum_kernel,
        out_shape=jax.ShapeDtypeStruct((2,) + arrived[0].shape, BF16),
        in_specs=[vmem()] * len(arrived),
        out_specs=vmem(),
        compiler_params=params(),
        name="sum_rows",
    )(*arrived)


def gram_kernel(heads_here, mine_ref, other_ref, bias_q_ref, bias_kv_ref, rows_ref, gram_ref):
    core = lax.rem(lax.axis_index("seq"), 2)
    wide = mine_ref.shape[2]
    for half in range(2):
        for ref, owner in ((mine_ref, core), (other_ref, 1 - core)):
            start = pl.multiple_of((half * 2 + owner) * wide, HD)
            rows_ref[:, pl.ds(start, wide)] = ref[half]
    spans = ((0, bias_q_ref), (bias_q_ref.shape[1], bias_kv_ref))
    for start, bias_ref in spans:
        here = pl.ds(start, bias_ref.shape[1])
        row = lax.broadcasted_iota(jnp.int32, (8, bias_ref.shape[1]), 0)
        block = rows_ref[64:WIRE, here].astype(F32)
        block = block + jnp.where(row == 1, bias_ref[...], 0.0)
        block = split_ends(block, row)
        block = block + jnp.where(row == 4, pltpu.roll(block, 3, 0), 0.0)
        rows_ref[64:WIRE, here] = block.astype(BF16)
    contract = (((1,), (1,)), ((), ()))
    queries = rows_ref[:, pl.ds(0, heads_here * HD)]
    gram_ref[0] = lax.dot_general(queries, queries, contract, preferred_element_type=F32)
    keys = jnp.concatenate(
        [rows_ref[:, pl.ds((heads_here + 2 * head) * HD, HD)] for head in range(heads_here)], axis=1
    )
    gram_ref[1] = lax.dot_general(keys, keys, contract, preferred_element_type=F32)


def gram_rows(mine, other, bias_q, bias_kv, heads_here):
    wide = mine.shape[2]
    return pl.pallas_call(
        functools.partial(gram_kernel, heads_here),
        out_shape=[
            jax.ShapeDtypeStruct((WIRE, BLOCKS * wide), BF16),
            jax.ShapeDtypeStruct((2, WIRE, WIRE), F32),
        ],
        in_specs=[vmem()] * 4,
        out_specs=[vmem()] * 2,
        compiler_params=params(),
        name="gram_rows",
    )(mine, other, bias_q, bias_kv)


def spread_kernel(mine_ref, other_ref, whole_ref, left_ref, turned_ref, spread_ref):
    tokens = mine_ref.shape[0]
    shards = whole_ref.shape[0]
    for part, ref in enumerate((mine_ref, other_ref)):
        rows = ref[...]
        pieces = []
        for shard in range(shards):
            weight = whole_ref[shard, 0:64].astype(BF16)
            pieces.append(
                jnp.dot(rows, weight, preferred_element_type=F32) + whole_ref[shard, 64:65]
            )
        average = sum(jnp.sum(piece, axis=1, keepdims=True) for piece in pieces) * (1.0 / D)
        squares = sum(
            jnp.sum((piece - average) * (piece - average), axis=1, keepdims=True)
            for piece in pieces
        )
        spread = jnp.sqrt(squares * (1.0 / D) + EPSILON)
        spread = jnp.broadcast_to(spread, (tokens, HD))
        first = spread.astype(BF16).astype(F32)
        lane = lax.broadcasted_iota(jnp.int32, (tokens, HD), 1)
        extra = jnp.where(
            (lane == 64) | (lane == 66),
            1.0,
            jnp.where(
                (lane == 65) | (lane == 67), first, jnp.where(lane == 68, spread - first, 0.0)
            ),
        )
        patch = jnp.concatenate([rows.astype(F32), jnp.zeros((tokens, HD - 64), F32)], axis=1)
        left = jnp.where(lane < 64, patch, extra)
        here = pl.ds(part * tokens, tokens)
        left_ref[here] = left.astype(BF16)
        turned_ref[:, here] = left.T.astype(BF16)
        spread_ref[here] = spread


def spread_rows(mine, other, whole):
    tokens = mine.shape[0]
    return pl.pallas_call(
        spread_kernel,
        out_shape=[
            jax.ShapeDtypeStruct((2 * tokens, HD), BF16),
            jax.ShapeDtypeStruct((HD, 2 * tokens), BF16),
            jax.ShapeDtypeStruct((2 * tokens, HD), F32),
        ],
        in_specs=[vmem()] * 3,
        out_specs=[vmem()] * 3,
        compiler_params=params(),
        name="spread_rows",
    )(mine, other, whole)


def heads_kernel(
    heads_here, left_ref, rows_ref, spread_ref, cosine_ref, sine_ref, gain_ref, q_ref, k_ref, v_ref
):
    tokens = q_ref.shape[0]
    left = left_ref[:, 0:WIRE]
    inverse = 1.0 / spread_ref[...]
    cosine, sine = cosine_ref[...], sine_ref[...]
    even = lax.broadcasted_iota(jnp.int32, cosine.shape, 1) % 2 == 0
    sine_even, sine_odd = jnp.where(even, -sine, 0.0), jnp.where(even, 0.0, sine)

    def rotate(values, count):
        back, ahead = pltpu.roll(values, HD - 1, 1), pltpu.roll(values, 1, 1)
        turned = values * cosine[:count] + back * sine_even[:count] + ahead * sine_odd[:count]
        return turned.astype(BF16)

    for head in range(heads_here):
        own = pl.ds(head * HD, HD)
        key_cols = pl.ds((heads_here + 2 * head) * HD, HD)
        value_cols = pl.ds((heads_here + 2 * head + 1) * HD, HD)
        query = jnp.dot(left[:tokens], rows_ref[:, own], preferred_element_type=F32)
        q_ref[:, own] = rotate(query * gain_ref[0:1, own], tokens)
        key = jnp.dot(left, rows_ref[:, key_cols], preferred_element_type=F32)
        k_ref[:, own] = rotate(key * gain_ref[1:2, own], 2 * tokens)
        value = jnp.dot(left, rows_ref[:, value_cols], preferred_element_type=F32)
        v_ref[:, own] = (value * inverse).astype(BF16)


def heads_rows(left, rows, spread, cosine, sine, gains, heads_here):
    both = left.shape[0]
    wide = heads_here * HD
    return pl.pallas_call(
        functools.partial(heads_kernel, heads_here),
        out_shape=[
            jax.ShapeDtypeStruct((both // 2, wide), BF16),
            jax.ShapeDtypeStruct((both, wide), BF16),
            jax.ShapeDtypeStruct((both, wide), BF16),
        ],
        in_specs=[vmem()] * 6,
        out_specs=[vmem()] * 3,
        compiler_params=params(),
        name="heads_rows",
    )(left, rows, spread, cosine, sine, gains)


def attend_kernel(
    heads_step,
    counts_ref,
    q_ref,
    k_ref,
    v_ref,
    left_ref,
    turned_ref,
    gram_ref,
    gram_other_ref,
    out_ref,
    query_scale,
    key_scale,
):
    tokens = q_ref.shape[0]
    place = lax.axis_index("seq")
    count_own = counts_ref[place]
    count_other = counts_ref[jnp.bitwise_xor(place, 1)]

    @pl.when(pl.program_id(0) == 0)
    def _():
        left = left_ref[0:tokens, 0:WIRE]
        turned = turned_ref[0:WIRE]
        gram_q, gram_k = [
            exact_pieces((gram_ref[which] + gram_other_ref[which]) * (1.0 / D), 3)
            for which in range(2)
        ]
        spun_q = sum(jnp.dot(left, piece, preferred_element_type=F32) for piece in gram_q)
        wide_left = left_ref[0:tokens].astype(F32)
        square_q = jnp.sum(spun_q * wide_left[:, 0:WIRE], axis=1, keepdims=True)
        spread_q = wide_left[:, 65:66] + wide_left[:, 68:69]
        query_scale[...] = jnp.broadcast_to(
            lax.rsqrt(square_q + EPSILON * spread_q * spread_q), query_scale.shape
        )
        spun_k = sum(jnp.dot(piece, turned, preferred_element_type=F32) for piece in gram_k)
        wide_turned = turned.astype(F32)
        square_k = jnp.sum(spun_k * wide_turned, axis=0, keepdims=True)
        spread_k = wide_turned[65:66] + wide_turned[68:69]
        key_scale[...] = jnp.broadcast_to(
            lax.rsqrt(square_k + EPSILON * spread_k * spread_k) * (1.0 / math.sqrt(HD)),
            key_scale.shape,
        )

    slot = lax.broadcasted_iota(jnp.int32, (1, 2 * tokens), 1)
    valid = slot < jnp.where(slot < tokens, count_own, tokens + count_other)
    row = lax.broadcasted_iota(jnp.int32, (tokens, HD), 0)
    contract = (((1,), (1,)), ((), ()))
    for head in range(heads_step):
        own = pl.ds(head * HD, HD)
        scores = lax.dot_general(q_ref[:, own], k_ref[:, own], contract, preferred_element_type=F32)
        scores = scores * query_scale[:, 0:1] * key_scale[0:1]
        weights = jnp.where(valid, jnp.exp(scores), 0.0)
        totals = jnp.sum(weights, axis=1, keepdims=True)
        result = jnp.dot(weights.astype(BF16), v_ref[:, own], preferred_element_type=F32)
        out_ref[:, own] = jnp.where(row < count_own, result / totals, 0.0).astype(BF16)


def attend_rows(counts, queries, keys, values, left, turned, gram, gram_other):
    tokens, wide = queries.shape
    heads_step = 2
    width = heads_step * HD
    whole = lambda *shape: pl.BlockSpec(shape, lambda step: (0,) * len(shape))
    return pl.pallas_call(
        functools.partial(attend_kernel, heads_step),
        out_shape=jax.ShapeDtypeStruct((tokens, wide), BF16),
        grid=(wide // width,),
        in_specs=[
            smem(),
            pl.BlockSpec((tokens, width), lambda step: (0, step)),
            pl.BlockSpec((2 * tokens, width), lambda step: (0, step)),
            pl.BlockSpec((2 * tokens, width), lambda step: (0, step)),
            whole(*left.shape),
            whole(*turned.shape),
            whole(*gram.shape),
            whole(*gram.shape),
        ],
        out_specs=pl.BlockSpec((tokens, width), lambda step: (0, step)),
        scratch_shapes=[pltpu.VMEM((tokens, HD), F32), pltpu.VMEM((8, 2 * tokens), F32)],
        compiler_params=params(),
        name="attend_rows",
    )(counts, queries, keys, values, left, turned, gram, gram_other)


def token_places(group_counts, member_ids, slot_ids, shape_row):
    before = jnp.cumsum(group_counts) - group_counts
    lookup = jnp.arange(GROUP, dtype=jnp.int32)[None, :] == member_ids[:, None]
    offset = jnp.sum(jnp.where(lookup, before[None, :], 0), axis=1)
    position = offset + slot_ids
    plane_size = shape_row[1] * shape_row[2]
    frame_pos = position // plane_size
    row_pos = position // shape_row[2] % shape_row[1]
    col_pos = position % shape_row[2]
    return (frame_pos, row_pos, col_pos)


def rotary_tables(frame_pos, row_pos, col_pos):
    other_pairs = HD // 6
    frame_pairs = HD // 2 - 2 * other_pairs
    pair_id = jnp.arange(HD, dtype=jnp.int32) // 2
    in_frame = pair_id < frame_pairs
    in_row = jnp.logical_and(pair_id >= frame_pairs, pair_id < frame_pairs + other_pairs)
    within = jnp.where(
        in_frame,
        pair_id,
        jnp.where(in_row, pair_id - frame_pairs, pair_id - frame_pairs - other_pairs),
    ).astype(F32)
    axis_span = jnp.where(in_frame, 2.0 * frame_pairs, 2.0 * other_pairs).astype(F32)
    inverse = jnp.exp(-(2.0 * within / axis_span) * math.log(10000.0))
    position = jnp.where(
        in_frame[None, :],
        frame_pos[:, None],
        jnp.where(in_row[None, :], row_pos[:, None], col_pos[:, None]),
    ).astype(F32)
    angles = position * inverse[None, :]
    return (jnp.cos(angles), jnp.sin(angles))


def shards(
    patches,
    clip_shape,
    shard_counts,
    patch_weight,
    patch_bias,
    time_mod,
    block_mod,
    w_query,
    query_bias,
    w_keyvalue,
    keyvalue_bias,
    norm_gain,
):
    tokens = patches.shape[0]
    heads_here = w_query.shape[1] // HD
    count = lax.axis_size("seq")
    halves = lax.axis_size("mp")
    place = lax.axis_index("seq")
    clips = time_mod.shape[0]
    rows = w_query.shape[0]
    padded = -(-rows // 16) * 16
    clips_sent = count // 4

    def pad_rows(values):
        return values if rows == padded else jnp.pad(values, ((0, padded - rows), (0, 0)))

    packed = pack_weights(pad_rows(w_query), pad_rows(w_keyvalue))
    pieces = []
    for flip in range(BLOCKS):
        piece = packed[flip] if flip == 0 else swap_bits(packed[flip], 2 * flip)
        pieces += [piece, swap_bits(piece, 1)]

    mods = (time_mod + block_mod).reshape(2 * clips, -1)
    features = patch_bias.shape[0]
    bundle = jnp.concatenate(
        [patch_weight.astype(F32), patch_bias[None], jnp.zeros((7, features), F32), mods]
    )
    whole = lax.all_gather(bundle, "mp", axis=0)
    other_patches = swap_bits(patches, 1)
    span = 8 * rows
    first = place // 8 * span
    part = lax.dynamic_slice(
        whole, (first // features, 0, first % features), (1, whole.shape[1], span)
    )[0]
    if rows != padded:
        part = jnp.pad(part.reshape(-1, 8, rows), ((0, 0), (0, 0), (0, padded - rows)))
        part = part.reshape(whole.shape[1], 8 * padded)
    whole = whole[:, 0:72]
    high, low = modulated_rows(
        whole, part[0:72], part[72:].reshape(clips, 2, -1), clips_sent
    )
    left, turned, spread = spread_rows(patches, other_patches, whole)

    products = product_rows(high, low, pieces, clips_sent)
    arrived = []
    for flip in range(clips_sent):
        pairs = []
        for source in range(count):
            rest, second, core = source // 4, source // 2 % 2, source % 2
            pairs.append((source, (rest ^ flip) * 4 + core * 2 + second))
        arrived.append(lax.ppermute(products[flip], "seq", pairs))

    clip_id = place // GROUP
    member = place % GROUP
    group_counts = lax.dynamic_slice_in_dim(shard_counts, clip_id * GROUP, GROUP, 0)
    shape_row = lax.dynamic_index_in_dim(clip_shape, clip_id, 0, keepdims=False)
    slots = jnp.arange(2 * tokens, dtype=jnp.int32)
    members = jnp.bitwise_xor(slots // tokens, member)
    cosine, sine = rotary_tables(
        *token_places(group_counts, members, slots % tokens, shape_row)
    )

    mine = sum_rows(arrived)
    other = swap_bits(mine, 1)
    columns, gram = gram_rows(
        mine, other, query_bias[None], keyvalue_bias[None], heads_here
    )
    gram_other = lax.ppermute(gram, "mp", [(i, (i + 1) % halves) for i in range(halves)])
    queries, keys, values = heads_rows(left, columns, spread, cosine, sine, norm_gain, heads_here)
    return attend_rows(shard_counts, queries, keys, values, left, turned, gram, gram_other)


def solution(mesh):
    return jax.shard_map(
        shards,
        mesh=mesh,
        in_specs=(
            P("seq", None),
            P(),
            P(),
            P(None, "mp"),
            P("mp"),
            P(None, None, "mp"),
            P(None, "mp"),
            P("seq", "mp"),
            P("mp"),
            P("seq", "mp"),
            P("mp"),
            P(None, "mp"),
        ),
        out_specs=P("seq", "mp"),
        check_vma=False,
    )
```

```python
import functools
import math

import jax
import jax.numpy as jnp
from jax import lax
from jax.experimental import pallas as pl
from jax.experimental.pallas import tpu as pltpu
from jax.sharding import PartitionSpec as P

D = 2560
HEADS = 20
HD = 128
GROUP = 2
EPSILON = 1e-06

BLOCKS = 4
WIRE = 72
STEP = 80
VMEM_LIMIT = 24 * 1024 * 1024
F32 = jnp.float32
BF16 = jnp.bfloat16


def params():
    return pltpu.CompilerParams(vmem_limit_bytes=VMEM_LIMIT)


def vmem():
    return pl.BlockSpec(memory_space=pltpu.VMEM)


def smem():
    return pl.BlockSpec(memory_space=pltpu.SMEM)


def swap_bits(value, mask):
    count = lax.axis_size("seq")
    return lax.ppermute(value, "seq", [(source, source ^ mask) for source in range(count)])


def exact_pieces(values, pieces):
    found = []
    for _ in range(pieces):
        piece = values.astype(BF16)
        found.append(piece)
        values = values - piece.astype(F32)
    return found


def block_chunks(chunks):
    whole = chunks // BLOCKS
    assert chunks - BLOCKS * whole == BLOCKS // 2
    return whole, BLOCKS * whole


def block_spans(block, chunks):
    whole, shared = block_chunks(chunks)
    return (block * whole * HD, whole * HD), ((shared + block // 2) * HD, HD)


def chip_block():
    return lax.rem(lax.div(lax.axis_index("seq"), 2), BLOCKS)


def after(value, *ready):
    anywhere = pl.BlockSpec(memory_space=pl.ANY)
    return pl.pallas_call(
        lambda *refs: None,
        out_shape=jax.ShapeDtypeStruct(value.shape, value.dtype),
        in_specs=[anywhere] * (1 + len(ready)),
        out_specs=anywhere,
        input_output_aliases={0: 0},
        compiler_params=pltpu.CompilerParams(vmem_limit_bytes=1024 * 1024),
        name="after",
    )(value, *ready)


def prepare_kernel(
    weight_ref, bias_ref, time_ref, block_ref, patches_ref, ready_ref, bundle_ref, copy_ref, mods
):
    clips = time_ref.shape[0]
    bundle_ref[0:64] = weight_ref[...]
    row = lax.broadcasted_iota(jnp.int32, (16, bundle_ref.shape[1]), 0)
    pieces = exact_pieces(bias_ref[...], 3)
    bundle_ref[64:80] = sum(
        jnp.where(row == which, piece.astype(F32), 0.0) for which, piece in enumerate(pieces)
    ).astype(BF16)
    for clip in range(clips):
        mods[pl.ds(2 * clip, 2)] = time_ref[clip] + block_ref[...]
    for which, piece in enumerate(exact_pieces(mods[...], 2)):
        bundle_ref[pl.ds(80 + 2 * clips * which, 2 * clips)] = piece
    copy_ref[...] = patches_ref[...]


def prepare_rows(weight, bias, time_mod, block_mod, patches, ready):
    clips, _, features = time_mod.shape
    return pl.pallas_call(
        prepare_kernel,
        out_shape=[
            jax.ShapeDtypeStruct((80 + 4 * clips, features), BF16),
            jax.ShapeDtypeStruct(patches.shape, BF16),
        ],
        in_specs=[vmem()] * 5 + [pl.BlockSpec(memory_space=pl.ANY)],
        out_specs=[vmem()] * 2,
        scratch_shapes=[pltpu.VMEM((2 * clips, features), F32)],
        compiler_params=params(),
        name="prepare_rows",
    )(weight, bias, time_mod, block_mod, patches, ready)


def bundle_bias(ref):
    return jnp.sum(ref[64:80].astype(F32), axis=0, keepdims=True)


def pack_kernel(wq_ref, wkv_ref, *refs):
    out_refs, (shared, sems, shared_sem) = refs[:-3], refs[-3:]
    rows, query_cols = wq_ref.shape
    chunks = (query_cols + wkv_ref.shape[1]) // HD
    whole, first_shared = block_chunks(chunks)
    mine = chip_block()

    def chunk_of(chunk):
        if chunk * HD < query_cols:
            return wq_ref.at[:, pl.ds(chunk * HD, HD)]
        return wkv_ref.at[:, pl.ds(chunk * HD - query_cols, HD)]

    copies = [
        pltpu.make_async_copy(chunk_of(first_shared + which), shared.at[which], shared_sem.at[which])
        for which in range(BLOCKS // 2)
    ]
    for copy in copies:
        copy.start()
    for flip in range(1, BLOCKS + 1):
        flip = flip % BLOCKS
        for block in range(BLOCKS):

            @pl.when(jnp.bitwise_xor(mine, flip) == block)
            def _(flip=flip, block=block):
                for chunk in range(whole):
                    pltpu.make_async_copy(
                        chunk_of(block * whole + chunk),
                        out_refs[flip].at[pl.ds(chunk * rows, rows)],
                        sems.at[flip],
                    ).start()

    for copy in copies:
        copy.wait()
    lane = lax.broadcasted_iota(jnp.int32, (rows // 2, HD), 1)
    for flip in range(BLOCKS):
        block = jnp.bitwise_xor(mine, flip)
        values = shared[lax.div(block, 2)].astype(F32)
        above, below = values[: rows // 2], values[rows // 2 :]
        even = jnp.where(lane < HD // 2, above, pltpu.roll(below, HD // 2, 1))
        odd = jnp.where(lane < HD // 2, pltpu.roll(above, HD // 2, 1), below)
        found = jnp.where(lax.rem(block, 2) == 0, even, odd)
        out_refs[flip][pl.ds(whole * rows, rows // 2)] = found.astype(BF16)
    for flip in range(BLOCKS):
        here = out_refs[flip].at[pl.ds(0, whole * rows)]
        pltpu.make_async_copy(here, here, sems.at[flip]).wait()


def pack_weights(w_query, w_keyvalue):
    rows = w_query.shape[0]
    whole, _ = block_chunks((w_query.shape[1] + w_keyvalue.shape[1]) // HD)
    return pl.pallas_call(
        pack_kernel,
        out_shape=[jax.ShapeDtypeStruct((whole * rows + rows // 2, HD), BF16)] * BLOCKS,
        in_specs=[pl.BlockSpec(memory_space=pltpu.HBM)] * 2,
        out_specs=[vmem()] * BLOCKS,
        scratch_shapes=[
            pltpu.VMEM((BLOCKS // 2, rows, HD), BF16),
            pltpu.SemaphoreType.DMA((BLOCKS,)),
            pltpu.SemaphoreType.DMA((BLOCKS // 2,)),
        ],
        compiler_params=params(),
        name="pack_weights",
    )(*[pltpu.with_memory_space_constraint(w, pltpu.HBM) for w in (w_query, w_keyvalue)])


def reorder_blocks(values, low):
    for bit in (2, 1, 0):
        count = 8 >> bit
        size = values.shape[1] // count
        blocks = [values[:, j * size : (j + 1) * size] for j in range(count)]
        swapped = jnp.concatenate([blocks[j ^ 1] for j in range(count)], axis=1)
        values = jnp.where(jnp.bitwise_and(low, 1 << bit) != 0, swapped, values)
    return values


def modulated_kernel(
    clips_sent, span, own_ref, other_ref, own_part_ref, other_part_ref, rows_ref, part
):
    place = lax.axis_index("seq")
    rest, core = lax.div(place, 4), lax.rem(place, 2)
    mods_rows = (own_ref.shape[0] - 80) // 2
    total = jnp.sum(own_ref[0:64].astype(F32), axis=1, keepdims=True)
    total = total + jnp.sum(other_ref[0:64].astype(F32), axis=1, keepdims=True)
    total_bias = jnp.sum(bundle_bias(own_ref) + bundle_bias(other_ref), axis=1, keepdims=True)
    owner = lax.div(lax.div(place, 8) * span, own_ref.shape[1])

    def unbundled(ref):
        mods = ref[80 : 80 + mods_rows].astype(F32) + ref[80 + mods_rows :].astype(F32)
        bias = jnp.broadcast_to(bundle_bias(ref), (8, mods.shape[1]))
        return jnp.concatenate([ref[0:64].astype(F32), bias, mods], axis=0)

    @pl.when(owner == lax.axis_index("mp"))
    def _():
        part[...] = unbundled(own_part_ref)

    @pl.when(owner != lax.axis_index("mp"))
    def _():
        part[...] = unbundled(other_part_ref)

    part[...] = reorder_blocks(part[...], jnp.bitwise_and(place, 7))
    centred = part[0:64] - total * (1.0 / D)
    centred_bias = part[64:65] - total_bias * (1.0 / D)
    row = lax.broadcasted_iota(jnp.int32, (STEP - 64, centred.shape[1]), 0)
    for flip in range(clips_sent):
        clip = jnp.bitwise_xor(rest, flip) * 2 + jnp.bitwise_xor(core, flip % 2)
        eight = part[pl.ds(pl.multiple_of(72 + 8 * lax.div(clip, 4), 8), 8)]
        first = 2 * lax.rem(clip, 4)
        shift = jnp.sum(jnp.where(row[:8] == first, eight, 0.0), axis=0, keepdims=True)
        scale = 1.0 + jnp.sum(jnp.where(row[:8] == first + 1, eight, 0.0), axis=0, keepdims=True)
        patch_rows = centred * scale
        extra = jnp.where(row == 0, centred_bias * scale, jnp.where(row == 1, shift, 0.0))
        rows_ref[pl.ds(flip * STEP, 64)] = patch_rows.astype(BF16)
        rows_ref[pl.ds(flip * STEP + 64, STEP - 64)] = extra.astype(BF16)


def modulated_rows(own, other, own_part, other_part, clips_sent, span):
    return pl.pallas_call(
        functools.partial(modulated_kernel, clips_sent, span),
        out_shape=jax.ShapeDtypeStruct((clips_sent * STEP, own_part.shape[1]), BF16),
        in_specs=[vmem()] * 4,
        out_specs=vmem(),
        scratch_shapes=[pltpu.VMEM((72 + (own.shape[0] - 80) // 2, own_part.shape[1]), F32)],
        compiler_params=params(),
        name="modulated_rows",
    )(own, other, own_part, other_part)


def free_lanes(lane, odd):
    return jnp.where(odd == 1, 0, HD // 2) == HD // 2 * lax.div(lane, HD // 2)


def doubled(values, lane, second):
    turned = pltpu.roll(values, HD // 2, 1)
    return jnp.where((lane < HD // 2) == (not second), values, turned)


def piece_chunks(refs, rows):
    whole = refs[0].shape[0] // rows
    for chunk in range(whole):
        yield jnp.concatenate([ref[pl.ds(chunk * rows, rows)] for ref in refs], axis=0)
    parts = []
    for ref in refs:
        half = ref[pl.ds(whole * rows, rows // 2)]
        parts += [half, pltpu.roll(half.astype(F32), HD // 2, 1).astype(BF16)]
    yield jnp.concatenate(parts, axis=0)


def piece_products(rows_here, refs, rows):
    chunks = list(piece_chunks(refs, rows))
    for chunk in range(0, len(chunks), 2):
        block = jnp.concatenate(chunks[chunk : chunk + 2], axis=1)
        yield chunk, jnp.dot(rows_here, block, preferred_element_type=F32)


def early_kernel(order, rows, rows_ref, *refs):
    out_ref = refs[-1]
    refs = [refs[order.index(block)] for block in sorted(order)]
    for chunk, total in piece_products(rows_ref[:, 0 : len(refs) * rows], refs, rows):
        out_ref[:, pl.ds(chunk * HD, 2 * HD)] = total


def early_rows(rows_here, pieces, rows):
    wide = (pieces[0].shape[0] // rows + 1) * HD
    return pl.pallas_call(
        functools.partial(early_kernel, list(pieces), rows),
        out_shape=jax.ShapeDtypeStruct((rows_here.shape[0], wide), F32),
        in_specs=[vmem()] * (1 + len(pieces)),
        out_specs=vmem(),
        compiler_params=params(),
        name="early_rows",
    )(rows_here, *pieces.values())


def product_kernel(clips_sent, order, rows, rows_ref, early_ref, *refs):
    refs, out_refs = refs[: len(order)], refs[len(order) :]
    refs = [refs[order.index(block)] for block in sorted(order)]
    done = rows_ref.shape[1] - len(order) * rows
    wide = early_ref.shape[1]
    tile = 2 * HD
    lane = lax.broadcasted_iota(jnp.int32, (8, HD), 1)
    row = lax.broadcasted_iota(jnp.int32, (8, HD), 0)
    odd = lax.rem(chip_block(), 2)
    ends = [[] for _ in range(clips_sent)]
    for first_chunk, total in piece_products(rows_ref[:, done:], refs, rows):
        start = first_chunk * HD
        columns = pl.ds(start, tile)
        total = total + early_ref[:, columns]
        for flip in range(clips_sent):
            base = flip * STEP
            for chunk in range(0, tile, HD):
                end = total[base + 64 : base + 72, chunk : chunk + HD]
                first = end.astype(BF16).astype(F32)
                end = first + pltpu.roll(end - first, 2, 0)
                low = doubled(end, lane, False)
                high = low if start + chunk + HD == wide else doubled(end, lane, True)
                ends[flip].append(jnp.where(row < 4, low, pltpu.roll(high, 4, 0)))
            patch_rows = total[base : base + 64]
            if start + tile == wide:
                wide_lane = lax.broadcasted_iota(jnp.int32, (64, HD), 1)
                last = jnp.where(
                    free_lanes(wide_lane, odd),
                    jnp.concatenate(ends[flip], axis=0),
                    doubled(patch_rows[:, tile - HD :], wide_lane, False),
                )
                patch_rows = jnp.concatenate([patch_rows[:, : tile - HD], last], axis=1)
            out_refs[flip][:, columns] = patch_rows.astype(BF16)


def product_rows(rows_here, early, pieces, clips_sent, rows):
    return pl.pallas_call(
        functools.partial(product_kernel, clips_sent, list(pieces), rows),
        out_shape=[jax.ShapeDtypeStruct((64, early.shape[1]), BF16)] * clips_sent,
        in_specs=[vmem()] * (2 + len(pieces)),
        out_specs=[vmem()] * clips_sent,
        compiler_params=params(),
        name="product_rows",
    )(rows_here, early, *pieces.values())


def split_ends(ends, row):
    ends = jnp.where(row < 2, ends + pltpu.roll(ends, 6, 0), 0.0)
    first = ends.astype(BF16).astype(F32)
    return first + pltpu.roll(ends - first, 2, 0)


def near_core(half):
    place = lax.axis_index("seq")
    core, low = lax.rem(place, 2), lax.rem(lax.div(place, 4), 2)
    return jnp.bitwise_xor(core, jnp.bitwise_xor(low, half))


def sum_kernel(flips, query_cols, pair_cols, *refs):
    in_refs, bias_ref = refs[: len(flips)], refs[len(flips)]
    out_ref, gram_ref, gram_sent_ref = refs[-3:]
    wide = out_ref.shape[2] - HD
    chunks = wide // HD
    own = lax.rem(lax.div(lax.axis_index("seq"), 4), 2)
    row = lax.broadcasted_iota(jnp.int32, (8, wide), 0)
    lane = lax.broadcasted_iota(jnp.int32, (1, wide), 1)
    chunk_lane = lax.broadcasted_iota(jnp.int32, (64, HD), 1)
    contract = (((1,), (1,)), ((), ()))
    grams = [jnp.zeros((WIRE, WIRE), F32)] * 2
    for parity in range(2):
        half = jnp.bitwise_xor(own, parity)
        odd = near_core(half)
        total = sum(ref[...].astype(F32) for ref, flip in zip(in_refs, flips) if flip % 2 == parity)
        last = total[:, wide - HD :]
        free = free_lanes(chunk_lane, odd)
        kept = jnp.where(free, last, pltpu.roll(last, HD // 2, 1))
        ends = []
        for chunk in range(chunks):
            eight = kept[8 * chunk : 8 * chunk + 8]
            ends.append(jnp.where(chunk_lane[:8] < HD // 2, eight, pltpu.roll(eight, 4, 0)))
        ends[-1] = kept[64 - 8 :]
        ends = jnp.where(row < 4, jnp.concatenate(ends, axis=1), 0.0)
        first = pl.multiple_of((half * 2 + odd) * wide, HD)
        ends = ends + jnp.where(row == 1, bias_ref[:, pl.ds(first, wide)], 0.0)
        ends = split_ends(ends, row)
        ends = ends + jnp.where(row == 4, pltpu.roll(ends, 3, 0), 0.0)
        rows = jnp.concatenate([total, ends], axis=0).astype(BF16)
        out_ref[half, :, 0:wide] = rows
        column = lane + (half * 2 + odd) * (wide - HD)
        tail = lane - (wide - HD)
        in_tail = tail >= 0
        column = jnp.where(in_tail, tail + BLOCKS * (wide - HD) + half * HD, column)
        held = jnp.logical_or(lane < wide - HD, lax.div(tail, HD // 2) == odd)
        pair = column - query_cols
        is_key = (pair >= 0) & (lax.rem(pair, 2 * HD) < HD)
        for which, keep in enumerate((pair < 0, is_key)):
            keep = jnp.where(keep, 1.0, 0.0) * jnp.where(held, 1.0, 0.0)
            kept = jnp.where(keep > 0.0, rows.astype(F32), 0.0).astype(BF16)
            grams[which] += lax.dot_general(kept, kept, contract, preferred_element_type=F32)
    row = lax.broadcasted_iota(jnp.int32, (WIRE, WIRE), 0)
    column = lax.broadcasted_iota(jnp.int32, (WIRE, WIRE), 1)
    both = jnp.where(
        row < column, 2.0 * grams[0], jnp.where(row == column, grams[0], 2.0 * grams[1])
    )
    diagonal = jnp.sum(jnp.where(row == column, grams[1], 0.0), axis=1, keepdims=True)
    gram_ref[:, 0:WIRE] = both
    gram_ref[:, WIRE:] = jnp.broadcast_to(diagonal, (WIRE, HD - WIRE))
    gram_sent_ref[...] = gram_ref[...].astype(BF16)
    for place, piece in enumerate(exact_pieces(gram_ref[...], 2)):
        out_ref[place, :, pl.ds(wide, HD)] = piece


def gram_halves(gram):
    row = lax.broadcasted_iota(jnp.int32, (WIRE, WIRE), 0)
    column = lax.broadcasted_iota(jnp.int32, (WIRE, WIRE), 1)
    both = gram[:, 0:WIRE]
    queries = jnp.where(row <= column, both, 0.0)
    keys = jnp.where(row > column, both, jnp.where(row == column, gram[:, WIRE : WIRE + 1], 0.0))
    return queries, keys


def sum_rows(arrived, bias, query_cols, pair_cols, ready):
    wide = next(iter(arrived.values())).shape[1]
    anywhere = pl.BlockSpec(memory_space=pl.ANY)
    return pl.pallas_call(
        functools.partial(sum_kernel, list(arrived), query_cols, pair_cols),
        out_shape=[
            jax.ShapeDtypeStruct((2, WIRE, wide + HD), BF16),
            jax.ShapeDtypeStruct((WIRE, HD), F32),
            jax.ShapeDtypeStruct((WIRE, HD), BF16),
        ],
        in_specs=[vmem()] * (len(arrived) + 1) + [anywhere] * len(ready),
        out_specs=[vmem()] * 3,
        compiler_params=params(),
        name="sum_rows",
    )(*arrived.values(), bias, *ready)


def rotary_tables(shape_ref, counts_ref, tokens):
    place = lax.axis_index("seq")
    clip, member = lax.div(place, GROUP), lax.rem(place, GROUP)
    height, width = shape_ref[clip, 1], shape_ref[clip, 2]
    first_count = counts_ref[clip * GROUP]
    slot = lax.broadcasted_iota(jnp.int32, (GROUP * tokens, HD), 0)
    own = slot < tokens
    offset = jnp.where(own, member * first_count, (1 - member) * first_count - tokens)
    position = (slot + offset).astype(F32)

    def quotient(values, divisor):
        return jnp.floor((values + 0.5) / divisor.astype(F32))

    line = quotient(position, width)
    frame = quotient(position, height * width)
    row = line - frame * height.astype(F32)
    column = position - line * width.astype(F32)

    other_pairs = HD // 6
    frame_pairs = HD // 2 - 2 * other_pairs
    lane = lax.broadcasted_iota(jnp.int32, (1, HD), 1)
    pair = lax.rem(lane, HD // 2)
    in_frame = pair < frame_pairs
    in_row = pair < frame_pairs + other_pairs
    before = jnp.where(in_frame, 0, jnp.where(in_row, frame_pairs, frame_pairs + other_pairs))
    span = jnp.where(in_frame, 2.0 * frame_pairs, 2.0 * other_pairs)
    inverse = jnp.exp(-(2.0 * (pair - before).astype(F32) / span) * math.log(10000.0))
    angles = jnp.where(in_frame, frame, jnp.where(in_row, row, column)) * inverse
    return jnp.cos(angles), jnp.sin(angles) * jnp.where(lane < HD // 2, -1.0, 1.0)


def pairs_apart():
    source = lax.broadcasted_iota(jnp.int32, (HD, HD), 0)
    lane = lax.broadcasted_iota(jnp.int32, (HD, HD), 1)
    wanted = 2 * lax.rem(lane, HD // 2) + lax.div(lane, HD // 2)
    return jnp.where(source == wanted, 1.0, 0.0).astype(BF16)


def spread_kernel(
    shape_ref,
    counts_ref,
    mine_ref,
    other_ref,
    here_ref,
    there_ref,
    gain_ref,
    bias_q_ref,
    bias_kv_ref,
    ready_ref,
    left_ref,
    turned_ref,
    spread_ref,
    cosine_ref,
    sine_ref,
    gain_apart_ref,
    bias_ref,
):
    tokens = mine_ref.shape[0]
    query_cols, pair_cols = bias_q_ref.shape[1], bias_kv_ref.shape[1]
    place = 0
    for block in range(BLOCKS):
        for first, size in block_spans(block, (query_cols + pair_cols) // HD):
            for ref, low in ((bias_q_ref, 0), (bias_kv_ref, query_cols)):
                start, stop = max(first, low), min(first + size, low + ref.shape[1])
                if start < stop:
                    here = pl.ds(place + start - first, stop - start)
                    values = ref[:, pl.ds(start - low, stop - start)]
                    bias_ref[:, here] = jnp.broadcast_to(values, (8, stop - start))
            place += size
    apart = pairs_apart()
    for head in range(gain_ref.shape[1] // HD):
        own = pl.ds(head * HD, HD)
        for which in range(2):
            gain = jnp.broadcast_to(gain_ref[which : which + 1, own], (8, HD))
            gain_apart_ref[which, :, own] = sum(
                jnp.dot(piece, apart, preferred_element_type=F32)
                for piece in exact_pieces(gain, 3)
            )
    cosine_ref[...], sine_ref[...] = rotary_tables(shape_ref, counts_ref, tokens)
    for part, ref in enumerate((mine_ref, other_ref)):
        rows = ref[...]
        pieces = []
        for half_ref in (here_ref, there_ref):
            pieces.append(
                jnp.dot(rows, half_ref[0:64], preferred_element_type=F32) + bundle_bias(half_ref)
            )
        average = sum(jnp.sum(piece, axis=1, keepdims=True) for piece in pieces) * (1.0 / D)
        squares = sum(
            jnp.sum((piece - average) * (piece - average), axis=1, keepdims=True)
            for piece in pieces
        )
        spread = jnp.sqrt(squares * (1.0 / D) + EPSILON)
        spread = jnp.broadcast_to(spread, (tokens, HD))
        first = spread.astype(BF16).astype(F32)
        lane = lax.broadcasted_iota(jnp.int32, (tokens, HD), 1)
        extra = jnp.where(
            (lane == 64) | (lane == 66),
            1.0,
            jnp.where(
                (lane == 65) | (lane == 67), first, jnp.where(lane == 68, spread - first, 0.0)
            ),
        )
        patch = jnp.concatenate([rows.astype(F32), jnp.zeros((tokens, HD - 64), F32)], axis=1)
        left = jnp.where(lane < 64, patch, extra)
        here = pl.ds(part * tokens, tokens)
        left_ref[here] = left.astype(BF16)
        turned_ref[:, here] = left.T.astype(BF16)
        spread_ref[here] = spread


def spread_rows(clip_shape, shard_counts, mine, other, here, there, gains, biases, ready):
    tokens = mine.shape[0]
    return pl.pallas_call(
        spread_kernel,
        out_shape=[
            jax.ShapeDtypeStruct((2 * tokens, HD), BF16),
            jax.ShapeDtypeStruct((HD, 2 * tokens), BF16),
        ]
        + [jax.ShapeDtypeStruct((2 * tokens, HD), F32)] * 3
        + [jax.ShapeDtypeStruct((2, 8, gains.shape[1]), F32)]
        + [jax.ShapeDtypeStruct((8, BLOCKS * ready.shape[1]), F32)],
        in_specs=[smem()] * 2 + [vmem()] * 7 + [pl.BlockSpec(memory_space=pl.ANY)],
        out_specs=[vmem()] * 7,
        compiler_params=params(),
        name="spread_rows",
    )(clip_shape, shard_counts, mine, other, here, there, gains, *biases, ready)


def heads_kernel(
    heads_here,
    counts_ref,
    left_ref,
    mine_ref,
    theirs_ref,
    spread_ref,
    cosine_ref,
    sine_ref,
    gain_ref,
    q_ref,
    k_ref,
    v_ref,
    rows,
):
    tokens = q_ref.shape[0]
    whole, shared = block_chunks(3 * heads_here)
    lane = lax.broadcasted_iota(jnp.int32, (WIRE, HD), 1)
    for half in range(2):
        near = near_core(half)
        for ref, core in ((mine_ref, near), (theirs_ref, 1 - near)):
            for chunk in range(whole):
                columns = ref[half, :, chunk * HD : (chunk + 1) * HD]
                rows[(half * 2 + core) * whole + chunk, 0:WIRE] = columns
        last = pl.ds(whole * HD, HD)
        mine, theirs = mine_ref[half, :, last].astype(F32), theirs_ref[half, :, last].astype(F32)
        columns = jnp.where(free_lanes(lane, near), theirs, mine)
        rows[shared + half, 0:WIRE] = columns.astype(BF16)
    place = lax.axis_index("seq")
    count_own, count_other = counts_ref[place], counts_ref[jnp.bitwise_xor(place, 1)]
    slot = lax.broadcasted_iota(jnp.int32, (2 * tokens, HD), 0)
    valid = slot < jnp.where(slot < tokens, count_own, tokens + count_other)
    left = left_ref[:, 0:WIRE]
    inverse = jnp.where(valid, 1.0 / spread_ref[...], 0.0)
    turned = list(range(heads_here)) + [heads_here + 2 * head for head in range(heads_here)]
    together = jnp.concatenate([rows[chunk] for chunk in turned], axis=0)
    together = jnp.dot(together, pairs_apart(), preferred_element_type=F32).astype(BF16)

    def projected(first, second, count):
        weight = jnp.concatenate([first, second], axis=1)
        found = jnp.dot(left[:count], weight, preferred_element_type=F32)
        return found[:, :HD], found[:, HD:]

    def rotated(values, gain, count):
        values = values * gain
        return values * cosine_ref[:count] + pltpu.roll(values, HD // 2, 1) * sine_ref[:count]

    def apart(index):
        return together[index * STEP : index * STEP + WIRE]

    for head in range(0, heads_here, 2):
        pair = (head, head + 1)
        for turn, found in zip(pair, projected(*[apart(turn) for turn in pair], tokens)):
            own = pl.ds(turn * HD, HD)
            q_ref[:, own] = rotated(found, gain_ref[0, 0:1, own], tokens)
        weights = [apart(heads_here + turn) for turn in pair]
        for turn, found in zip(pair, projected(*weights, 2 * tokens)):
            own = pl.ds(turn * HD, HD)
            k_ref[:, own] = rotated(found, gain_ref[1, 0:1, own], 2 * tokens).astype(BF16)
        weights = [rows[heads_here + 2 * turn + 1, 0:WIRE] for turn in pair]
        for turn, found in zip(pair, projected(*weights, 2 * tokens)):
            v_ref[:, pl.ds(turn * HD, HD)] = (found * inverse).astype(BF16)


def heads_rows(counts, left, mine, theirs, spread, cosine, sine, gains, heads_here):
    both = left.shape[0]
    wide = heads_here * HD
    return pl.pallas_call(
        functools.partial(heads_kernel, heads_here),
        out_shape=[
            jax.ShapeDtypeStruct((both // 2, wide), F32),
            jax.ShapeDtypeStruct((both, wide), BF16),
            jax.ShapeDtypeStruct((both, wide), BF16),
        ],
        in_specs=[smem()] + [vmem()] * 7,
        out_specs=[vmem()] * 3,
        scratch_shapes=[pltpu.VMEM((3 * heads_here, STEP, HD), BF16)],
        compiler_params=params(),
        name="heads_rows",
    )(counts, left, mine, theirs, spread, cosine, sine, gains)


def attend_kernel(
    heads_here, counts_ref, q_ref, k_ref, v_ref, left_ref, turned_ref, theirs_ref, *refs
):
    gram_refs, (out_ref, found, sems) = refs[:-3], refs[-3:]
    tokens = q_ref.shape[0]
    place = lax.axis_index("seq")
    count_own, count_other = counts_ref[place], counts_ref[jnp.bitwise_xor(place, 1)]

    left = left_ref[0:tokens, 0:WIRE]
    turned = turned_ref[0:WIRE]
    last = theirs_ref.shape[2] - HD
    gram = sum(ref[...].astype(F32) for ref in gram_refs)
    for place in range(2):
        gram = gram + theirs_ref[place, :, last:].astype(F32)
    gram = gram * (1.0 / D)
    gram_q, gram_k = [exact_pieces(values, 2) for values in gram_halves(gram)]
    spun_q = sum(jnp.dot(left, piece, preferred_element_type=F32) for piece in gram_q)
    wide_left = left_ref[0:tokens].astype(F32)
    square_q = jnp.sum(spun_q * wide_left[:, 0:WIRE], axis=1, keepdims=True)
    spread_q = wide_left[:, 65:66] + wide_left[:, 68:69]
    scale_q = lax.rsqrt(square_q + EPSILON * spread_q * spread_q) * (
        math.log2(math.e) / math.sqrt(HD)
    )
    scale_q = jnp.broadcast_to(scale_q, (tokens, HD))
    spun_k = sum(jnp.dot(piece, turned, preferred_element_type=F32) for piece in gram_k)
    wide_turned = turned.astype(F32)
    square_k = jnp.sum(spun_k * wide_turned, axis=0, keepdims=True)
    spread_k = wide_turned[65:66] + wide_turned[68:69]
    scale_k = lax.rsqrt(square_k + EPSILON * spread_k * spread_k)
    slot = lax.broadcasted_iota(jnp.int32, (1, 2 * tokens), 1)
    valid = slot < jnp.where(slot < tokens, count_own, tokens + count_other)
    scale_k = jnp.where(valid, scale_k, 0.0)

    slot = lax.broadcasted_iota(jnp.int32, (2 * tokens, HD), 0)
    valid = slot < jnp.where(slot < tokens, count_own, tokens + count_other)
    ones = jnp.where(valid, 1.0, 0.0).astype(BF16)
    row = lax.broadcasted_iota(jnp.int32, (tokens, HD), 0)
    contract = (((1,), (1,)), ((), ()))

    def scores_of(head):
        own = pl.ds(head * HD, HD)
        query = (q_ref[:, own] * scale_q).astype(BF16)
        return lax.dot_general(query, k_ref[:, own], contract, preferred_element_type=F32)

    copies = []
    scores = scores_of(0)
    for head in range(heads_here):
        own = pl.ds(head * HD, HD)
        later = scores_of(head + 1) if head + 1 < heads_here else None
        weights = jnp.exp2(scores * scale_k).astype(BF16)
        values = jnp.concatenate([v_ref[:, own], ones], axis=1)
        result = jnp.dot(weights, values, preferred_element_type=F32)
        result = result[:, 0:HD] / result[:, HD:]
        found[:, own] = jnp.where(row < count_own, result, 0.0).astype(BF16)
        copies.append(pltpu.make_async_copy(found.at[:, own], out_ref.at[:, own], sems.at[head]))
        copies[-1].start()
        scores = later
    for copy in copies:
        copy.wait()


def attend_rows(counts, queries, keys, values, left, turned, theirs, grams):
    heads_here = queries.shape[1] // HD
    return pl.pallas_call(
        functools.partial(attend_kernel, heads_here),
        out_shape=jax.ShapeDtypeStruct(queries.shape, BF16),
        in_specs=[smem()] + [vmem()] * (6 + len(grams)),
        out_specs=pl.BlockSpec(memory_space=pl.ANY),
        scratch_shapes=[
            pltpu.VMEM(queries.shape, BF16),
            pltpu.SemaphoreType.DMA((heads_here,)),
        ],
        compiler_params=params(),
        name="attend_rows",
    )(counts, queries, keys, values, left, turned, theirs, *grams)


def shards(
    patches,
    clip_shape,
    shard_counts,
    patch_weight,
    patch_bias,
    time_mod,
    block_mod,
    w_query,
    query_bias,
    w_keyvalue,
    keyvalue_bias,
    norm_gain,
):
    tokens = patches.shape[0]
    heads_here = w_query.shape[1] // HD
    count = lax.axis_size("seq")
    halves = lax.axis_size("mp")
    place = lax.axis_index("seq")
    clips = time_mod.shape[0]
    rows = w_query.shape[0]
    padded = -(-rows // 16) * 16
    clips_sent = count // 4

    def pad_rows(values):
        return values if rows == padded else jnp.pad(values, ((0, padded - rows), (0, 0)))

    packed = pack_weights(pad_rows(w_query), pad_rows(w_keyvalue))
    pieces = [packed[0]] + [swap_bits(packed[flip], 2 * flip) for flip in range(1, BLOCKS)]
    first_swapped = swap_bits(packed[0], 1)

    features = patch_bias.shape[0]
    own, own_patches = prepare_rows(
        patch_weight, patch_bias[None], time_mod, block_mod, patches, first_swapped
    )
    other = lax.ppermute(own, "mp", [(i, (i + 1) % halves) for i in range(halves)])
    other_patches = swap_bits(own_patches, 1)
    span = 8 * rows

    def group_part(values):
        if span == features and rows == padded:
            return values
        values = lax.dynamic_slice_in_dim(values, place // 8 * span % features, span, 1)
        values = jnp.pad(
            values.reshape(-1, 8, rows), ((0, 0), (0, 0), (0, padded - rows))
        )
        return values.reshape(-1, 8 * padded)

    rows_here = modulated_rows(
        own, other, group_part(own), group_part(other), clips_sent, span
    )
    placed = {0: packed[0], 1: first_swapped}
    for flip in reversed(range(1, BLOCKS)):
        piece = after(pieces[flip], rows_here, other_patches)
        placed[2 * flip], placed[2 * flip + 1] = piece, swap_bits(piece, 1)
    first = {order: placed.pop(order) for order in (6, 4, 5, 2, 3, 0, 1)}
    early = early_rows(rows_here, first, padded)

    products = product_rows(rows_here, early, placed, clips_sent, padded)
    arrived = {}
    for flip in reversed(range(clips_sent)):
        pairs = []
        for source in range(count):
            rest, second, core = source // 4, source // 2 % 2, source % 2
            turn = flip % 2
            pairs.append((source, (rest ^ flip) * 4 + (core ^ turn) * 2 + (second ^ turn)))
        arrived[flip] = lax.ppermute(products[flip], "seq", pairs)
    biases = (query_bias[None], keyvalue_bias[None])
    left, turned, spread, cosine, sine, gains, bias = spread_rows(
        clip_shape,
        shard_counts,
        own_patches,
        other_patches,
        own,
        other,
        norm_gain,
        biases,
        products[0],
    )

    mine, gram, gram_sent = sum_rows(arrived, bias, w_query.shape[1], w_keyvalue.shape[1], (left,))
    theirs = swap_bits(mine, 1)
    far_mp = [(i, (i + 1) % halves) for i in range(halves)]
    far_both = [
        (core * halves + i, (core ^ 1) * halves + j) for core in range(count) for i, j in far_mp
    ]
    grams = (
        gram,
        lax.ppermute(gram_sent, "mp", far_mp),
        lax.ppermute(gram_sent, ("seq", "mp"), far_both),
    )
    queries, keys, values = heads_rows(
        shard_counts, left, mine, theirs, spread, cosine, sine, gains, heads_here
    )
    return attend_rows(shard_counts, queries, keys, values, left, turned, theirs, grams)


def solution(mesh):
    return jax.shard_map(
        shards,
        mesh=mesh,
        in_specs=(
            P("seq", None),
            P(),
            P(),
            P(None, "mp"),
            P("mp"),
            P(None, None, "mp"),
            P(None, "mp"),
            P("seq", "mp"),
            P("mp"),
            P("seq", "mp"),
            P("mp"),
            P(None, "mp"),
        ),
        out_specs=P("seq", "mp"),
        check_vma=False,
    )
```

```python
import functools
import math

import jax
import jax.numpy as jnp
from jax import lax
from jax.experimental import pallas as pl
from jax.experimental.pallas import tpu as pltpu
from jax.sharding import PartitionSpec as P

D = 2560
HEADS = 20
HD = 128
GROUP = 2
EPSILON = 1e-06

BLOCKS = 4
WIRE = 72
STEP = 80
VMEM_LIMIT = 24 * 1024 * 1024
F32 = jnp.float32
BF16 = jnp.bfloat16


def params():
    return pltpu.CompilerParams(vmem_limit_bytes=VMEM_LIMIT)


def vmem():
    return pl.BlockSpec(memory_space=pltpu.VMEM)


def smem():
    return pl.BlockSpec(memory_space=pltpu.SMEM)


def swap_bits(value, mask):
    count = lax.axis_size("seq")
    return lax.ppermute(value, "seq", [(source, source ^ mask) for source in range(count)])


def exact_pieces(values, pieces):
    found = []
    for _ in range(pieces):
        piece = values.astype(BF16)
        found.append(piece)
        values = values - piece.astype(F32)
    return found


def block_chunks(chunks):
    whole = chunks // BLOCKS
    assert chunks - BLOCKS * whole == BLOCKS // 2
    return whole, BLOCKS * whole


def block_spans(block, chunks):
    whole, shared = block_chunks(chunks)
    return (block * whole * HD, whole * HD), ((shared + block // 2) * HD, HD)


def chip_block():
    return lax.rem(lax.div(lax.axis_index("seq"), 2), BLOCKS)


def after(value, *ready):
    anywhere = pl.BlockSpec(memory_space=pl.ANY)
    return pl.pallas_call(
        lambda *refs: None,
        out_shape=jax.ShapeDtypeStruct(value.shape, value.dtype),
        in_specs=[anywhere] * (1 + len(ready)),
        out_specs=anywhere,
        input_output_aliases={0: 0},
        compiler_params=pltpu.CompilerParams(vmem_limit_bytes=1024 * 1024),
        name="after",
    )(value, *ready)


def prepare_kernel(
    weight_ref, bias_ref, time_ref, block_ref, patches_ref, ready_ref, bundle_ref, copy_ref, mods
):
    clips = time_ref.shape[0]
    bundle_ref[0:64] = weight_ref[...]
    row = lax.broadcasted_iota(jnp.int32, (16, bundle_ref.shape[1]), 0)
    pieces = exact_pieces(bias_ref[...], 3)
    bundle_ref[64:80] = sum(
        jnp.where(row == which, piece.astype(F32), 0.0) for which, piece in enumerate(pieces)
    ).astype(BF16)
    for clip in range(clips):
        mods[pl.ds(2 * clip, 2)] = time_ref[clip] + block_ref[...]
    for which, piece in enumerate(exact_pieces(mods[...], 2)):
        bundle_ref[pl.ds(80 + 2 * clips * which, 2 * clips)] = piece
    copy_ref[...] = patches_ref[...]


def prepare_rows(weight, bias, time_mod, block_mod, patches, ready):
    clips, _, features = time_mod.shape
    return pl.pallas_call(
        prepare_kernel,
        out_shape=[
            jax.ShapeDtypeStruct((80 + 4 * clips, features), BF16),
            jax.ShapeDtypeStruct(patches.shape, BF16),
        ],
        in_specs=[vmem()] * 5 + [pl.BlockSpec(memory_space=pl.ANY)],
        out_specs=[vmem()] * 2,
        scratch_shapes=[pltpu.VMEM((2 * clips, features), F32)],
        compiler_params=params(),
        name="prepare_rows",
    )(weight, bias, time_mod, block_mod, patches, ready)


def bundle_bias(ref):
    return jnp.sum(ref[64:80].astype(F32), axis=0, keepdims=True)


def pack_kernel(wq_ref, wkv_ref, *refs):
    out_refs, (shared, sems, shared_sem) = refs[:-3], refs[-3:]
    rows, query_cols = wq_ref.shape
    chunks = (query_cols + wkv_ref.shape[1]) // HD
    whole, first_shared = block_chunks(chunks)
    mine = chip_block()

    def chunk_of(chunk):
        if chunk * HD < query_cols:
            return wq_ref.at[:, pl.ds(chunk * HD, HD)]
        return wkv_ref.at[:, pl.ds(chunk * HD - query_cols, HD)]

    copies = [
        pltpu.make_async_copy(chunk_of(first_shared + which), shared.at[which], shared_sem.at[which])
        for which in range(BLOCKS // 2)
    ]
    for copy in copies:
        copy.start()
    for flip in range(1, BLOCKS + 1):
        flip = flip % BLOCKS
        for block in range(BLOCKS):

            @pl.when(jnp.bitwise_xor(mine, flip) == block)
            def _(flip=flip, block=block):
                for chunk in range(whole):
                    pltpu.make_async_copy(
                        chunk_of(block * whole + chunk),
                        out_refs[flip].at[pl.ds(chunk * rows, rows)],
                        sems.at[flip],
                    ).start()

    for copy in copies:
        copy.wait()
    lane = lax.broadcasted_iota(jnp.int32, (rows // 2, HD), 1)
    for flip in range(BLOCKS):
        block = jnp.bitwise_xor(mine, flip)
        values = shared[lax.div(block, 2)].astype(F32)
        above, below = values[: rows // 2], values[rows // 2 :]
        even = jnp.where(lane < HD // 2, above, pltpu.roll(below, HD // 2, 1))
        odd = jnp.where(lane < HD // 2, pltpu.roll(above, HD // 2, 1), below)
        found = jnp.where(lax.rem(block, 2) == 0, even, odd)
        out_refs[flip][pl.ds(whole * rows, rows // 2)] = found.astype(BF16)
    for flip in range(BLOCKS):
        here = out_refs[flip].at[pl.ds(0, whole * rows)]
        pltpu.make_async_copy(here, here, sems.at[flip]).wait()


def pack_weights(w_query, w_keyvalue):
    rows = w_query.shape[0]
    whole, _ = block_chunks((w_query.shape[1] + w_keyvalue.shape[1]) // HD)
    return pl.pallas_call(
        pack_kernel,
        out_shape=[jax.ShapeDtypeStruct((whole * rows + rows // 2, HD), BF16)] * BLOCKS,
        in_specs=[pl.BlockSpec(memory_space=pltpu.HBM)] * 2,
        out_specs=[vmem()] * BLOCKS,
        scratch_shapes=[
            pltpu.VMEM((BLOCKS // 2, rows, HD), BF16),
            pltpu.SemaphoreType.DMA((BLOCKS,)),
            pltpu.SemaphoreType.DMA((BLOCKS // 2,)),
        ],
        compiler_params=params(),
        name="pack_weights",
    )(*[pltpu.with_memory_space_constraint(w, pltpu.HBM) for w in (w_query, w_keyvalue)])


def reorder_blocks(values, low):
    for bit in (2, 1, 0):
        count = 8 >> bit
        size = values.shape[1] // count
        blocks = [values[:, j * size : (j + 1) * size] for j in range(count)]
        swapped = jnp.concatenate([blocks[j ^ 1] for j in range(count)], axis=1)
        values = jnp.where(jnp.bitwise_and(low, 1 << bit) != 0, swapped, values)
    return values


def modulated_kernel(
    clips_sent, span, own_ref, other_ref, own_part_ref, other_part_ref, rows_ref, rest_ref, part
):
    place = lax.axis_index("seq")
    rest, core = lax.div(place, 4), lax.rem(place, 2)
    mods_rows = (own_ref.shape[0] - 80) // 2
    total = jnp.sum(own_ref[0:64].astype(F32), axis=1, keepdims=True)
    total = total + jnp.sum(other_ref[0:64].astype(F32), axis=1, keepdims=True)
    total_bias = jnp.sum(bundle_bias(own_ref) + bundle_bias(other_ref), axis=1, keepdims=True)
    owner = lax.div(lax.div(place, 8) * span, own_ref.shape[1])

    def unbundled(ref):
        mods = ref[80 : 80 + mods_rows].astype(F32) + ref[80 + mods_rows :].astype(F32)
        bias = jnp.broadcast_to(bundle_bias(ref), (8, mods.shape[1]))
        return jnp.concatenate([ref[0:64].astype(F32), bias, mods], axis=0)

    @pl.when(owner == lax.axis_index("mp"))
    def _():
        part[...] = unbundled(own_part_ref)

    @pl.when(owner != lax.axis_index("mp"))
    def _():
        part[...] = unbundled(other_part_ref)

    part[...] = reorder_blocks(part[...], jnp.bitwise_and(place, 7))
    centred = part[0:64] - total * (1.0 / D)
    centred_bias = part[64:65] - total_bias * (1.0 / D)
    row = lax.broadcasted_iota(jnp.int32, (STEP - 64, centred.shape[1]), 0)
    for flip in range(clips_sent):
        clip = jnp.bitwise_xor(rest, flip) * 2 + jnp.bitwise_xor(core, flip % 2)
        eight = part[pl.ds(pl.multiple_of(72 + 8 * lax.div(clip, 4), 8), 8)]
        first = 2 * lax.rem(clip, 4)
        shift = jnp.sum(jnp.where(row[:8] == first, eight, 0.0), axis=0, keepdims=True)
        scale = 1.0 + jnp.sum(jnp.where(row[:8] == first + 1, eight, 0.0), axis=0, keepdims=True)
        patch_rows = centred * scale
        extra = jnp.where(row == 0, centred_bias * scale, jnp.where(row == 1, shift, 0.0))
        for start, values in ((0, patch_rows), (64, extra)):
            here = pl.ds(flip * STEP + start, values.shape[0])
            rows_ref[here], rest_ref[here] = exact_pieces(values, 2)


def modulated_rows(own, other, own_part, other_part, clips_sent, span):
    return pl.pallas_call(
        functools.partial(modulated_kernel, clips_sent, span),
        out_shape=[jax.ShapeDtypeStruct((clips_sent * STEP, own_part.shape[1]), BF16)] * 2,
        in_specs=[vmem()] * 4,
        out_specs=[vmem()] * 2,
        scratch_shapes=[pltpu.VMEM((72 + (own.shape[0] - 80) // 2, own_part.shape[1]), F32)],
        compiler_params=params(),
        name="modulated_rows",
    )(own, other, own_part, other_part)


def free_lanes(lane, odd):
    return jnp.where(odd == 1, 0, HD // 2) == HD // 2 * lax.div(lane, HD // 2)


def doubled(values, lane, second):
    turned = pltpu.roll(values, HD // 2, 1)
    return jnp.where((lane < HD // 2) == (not second), values, turned)


def piece_chunks(refs, rows):
    whole = refs[0].shape[0] // rows
    for chunk in range(whole):
        yield jnp.concatenate([ref[pl.ds(chunk * rows, rows)] for ref in refs], axis=0)
    parts = []
    for ref in refs:
        half = ref[pl.ds(whole * rows, rows // 2)]
        parts += [half, pltpu.roll(half.astype(F32), HD // 2, 1).astype(BF16)]
    yield jnp.concatenate(parts, axis=0)


def piece_products(rows_here, rest_here, refs, rows):
    chunks = list(piece_chunks(refs, rows))
    for chunk in range(0, len(chunks), 2):
        block = jnp.concatenate(chunks[chunk : chunk + 2], axis=1)
        total = jnp.dot(rows_here, block, preferred_element_type=F32)
        yield chunk, total + jnp.dot(rest_here, block, preferred_element_type=F32)


def early_kernel(order, rows, rows_ref, rest_ref, *refs):
    out_ref = refs[-1]
    refs = [refs[order.index(block)] for block in sorted(order)]
    used = len(refs) * rows
    for chunk, total in piece_products(rows_ref[:, :used], rest_ref[:, :used], refs, rows):
        out_ref[:, pl.ds(chunk * HD, 2 * HD)] = total


def early_rows(rows_here, rest_here, pieces, rows):
    wide = (pieces[0].shape[0] // rows + 1) * HD
    return pl.pallas_call(
        functools.partial(early_kernel, list(pieces), rows),
        out_shape=jax.ShapeDtypeStruct((rows_here.shape[0], wide), F32),
        in_specs=[vmem()] * (2 + len(pieces)),
        out_specs=vmem(),
        compiler_params=params(),
        name="early_rows",
    )(rows_here, rest_here, *pieces.values())


def product_kernel(clips_sent, order, rows, rows_ref, rest_ref, early_ref, *refs):
    refs, out_refs = refs[: len(order)], refs[len(order) :]
    refs = [refs[order.index(block)] for block in sorted(order)]
    done = rows_ref.shape[1] - len(order) * rows
    wide = early_ref.shape[1]
    tile = 2 * HD
    lane = lax.broadcasted_iota(jnp.int32, (8, HD), 1)
    row = lax.broadcasted_iota(jnp.int32, (8, HD), 0)
    odd = lax.rem(chip_block(), 2)
    ends = [[] for _ in range(clips_sent)]
    for first_chunk, total in piece_products(
        rows_ref[:, done:], rest_ref[:, done:], refs, rows
    ):
        start = first_chunk * HD
        columns = pl.ds(start, tile)
        total = total + early_ref[:, columns]
        for flip in range(clips_sent):
            base = flip * STEP
            for chunk in range(0, tile, HD):
                end = total[base + 64 : base + 72, chunk : chunk + HD]
                first = end.astype(BF16).astype(F32)
                end = first + pltpu.roll(end - first, 2, 0)
                low = doubled(end, lane, False)
                high = low if start + chunk + HD == wide else doubled(end, lane, True)
                ends[flip].append(jnp.where(row < 4, low, pltpu.roll(high, 4, 0)))
            patch_rows = total[base : base + 64]
            if start + tile == wide:
                wide_lane = lax.broadcasted_iota(jnp.int32, (64, HD), 1)
                last = jnp.where(
                    free_lanes(wide_lane, odd),
                    jnp.concatenate(ends[flip], axis=0),
                    doubled(patch_rows[:, tile - HD :], wide_lane, False),
                )
                patch_rows = jnp.concatenate([patch_rows[:, : tile - HD], last], axis=1)
            out_refs[flip][:, columns] = patch_rows.astype(BF16)


def product_rows(rows_here, rest_here, early, pieces, clips_sent, rows):
    return pl.pallas_call(
        functools.partial(product_kernel, clips_sent, list(pieces), rows),
        out_shape=[jax.ShapeDtypeStruct((64, early.shape[1]), BF16)] * clips_sent,
        in_specs=[vmem()] * (3 + len(pieces)),
        out_specs=[vmem()] * clips_sent,
        compiler_params=params(),
        name="product_rows",
    )(rows_here, rest_here, early, *pieces.values())


def split_ends(ends, row):
    ends = jnp.where(row < 2, ends + pltpu.roll(ends, 6, 0), 0.0)
    first = ends.astype(BF16).astype(F32)
    return first + pltpu.roll(ends - first, 2, 0)


def near_core(half):
    place = lax.axis_index("seq")
    core, low = lax.rem(place, 2), lax.rem(lax.div(place, 4), 2)
    return jnp.bitwise_xor(core, jnp.bitwise_xor(low, half))


def sum_kernel(flips, query_cols, pair_cols, *refs):
    in_refs, bias_ref = refs[: len(flips)], refs[len(flips)]
    out_ref, gram_ref, gram_sent_ref = refs[-3:]
    wide = out_ref.shape[2] - HD
    chunks = wide // HD
    own = lax.rem(lax.div(lax.axis_index("seq"), 4), 2)
    row = lax.broadcasted_iota(jnp.int32, (8, wide), 0)
    lane = lax.broadcasted_iota(jnp.int32, (1, wide), 1)
    chunk_lane = lax.broadcasted_iota(jnp.int32, (64, HD), 1)
    contract = (((1,), (1,)), ((), ()))
    grams = [jnp.zeros((WIRE, WIRE), F32)] * 2
    for parity in range(2):
        half = jnp.bitwise_xor(own, parity)
        odd = near_core(half)
        total = sum(ref[...].astype(F32) for ref, flip in zip(in_refs, flips) if flip % 2 == parity)
        last = total[:, wide - HD :]
        free = free_lanes(chunk_lane, odd)
        kept = jnp.where(free, last, pltpu.roll(last, HD // 2, 1))
        ends = []
        for chunk in range(chunks):
            eight = kept[8 * chunk : 8 * chunk + 8]
            ends.append(jnp.where(chunk_lane[:8] < HD // 2, eight, pltpu.roll(eight, 4, 0)))
        ends[-1] = kept[64 - 8 :]
        ends = jnp.where(row < 4, jnp.concatenate(ends, axis=1), 0.0)
        first = pl.multiple_of((half * 2 + odd) * wide, HD)
        ends = ends + jnp.where(row == 1, bias_ref[:, pl.ds(first, wide)], 0.0)
        ends = split_ends(ends, row)
        ends = ends + jnp.where(row == 4, pltpu.roll(ends, 3, 0), 0.0)
        rows = jnp.concatenate([total, ends], axis=0).astype(BF16)
        out_ref[half, :, 0:wide] = rows
        column = lane + (half * 2 + odd) * (wide - HD)
        tail = lane - (wide - HD)
        in_tail = tail >= 0
        column = jnp.where(in_tail, tail + BLOCKS * (wide - HD) + half * HD, column)
        held = jnp.logical_or(lane < wide - HD, lax.div(tail, HD // 2) == odd)
        pair = column - query_cols
        is_key = (pair >= 0) & (lax.rem(pair, 2 * HD) < HD)
        for which, keep in enumerate((pair < 0, is_key)):
            keep = jnp.where(keep, 1.0, 0.0) * jnp.where(held, 1.0, 0.0)
            kept = jnp.where(keep > 0.0, rows.astype(F32), 0.0).astype(BF16)
            grams[which] += lax.dot_general(kept, kept, contract, preferred_element_type=F32)
    row = lax.broadcasted_iota(jnp.int32, (WIRE, WIRE), 0)
    column = lax.broadcasted_iota(jnp.int32, (WIRE, WIRE), 1)
    both = jnp.where(
        row < column, 2.0 * grams[0], jnp.where(row == column, grams[0], 2.0 * grams[1])
    )
    diagonal = jnp.sum(jnp.where(row == column, grams[1], 0.0), axis=1, keepdims=True)
    gram_ref[:, 0:WIRE] = both
    gram_ref[:, WIRE:] = jnp.broadcast_to(diagonal, (WIRE, HD - WIRE))
    gram_sent_ref[...] = gram_ref[...].astype(BF16)
    for place, piece in enumerate(exact_pieces(gram_ref[...], 2)):
        out_ref[place, :, pl.ds(wide, HD)] = piece


def gram_halves(gram):
    row = lax.broadcasted_iota(jnp.int32, (WIRE, WIRE), 0)
    column = lax.broadcasted_iota(jnp.int32, (WIRE, WIRE), 1)
    both = gram[:, 0:WIRE]
    queries = jnp.where(row <= column, both, 0.0)
    keys = jnp.where(row > column, both, jnp.where(row == column, gram[:, WIRE : WIRE + 1], 0.0))
    return queries, keys


def sum_rows(arrived, bias, query_cols, pair_cols, ready):
    wide = next(iter(arrived.values())).shape[1]
    anywhere = pl.BlockSpec(memory_space=pl.ANY)
    return pl.pallas_call(
        functools.partial(sum_kernel, list(arrived), query_cols, pair_cols),
        out_shape=[
            jax.ShapeDtypeStruct((2, WIRE, wide + HD), BF16),
            jax.ShapeDtypeStruct((WIRE, HD), F32),
            jax.ShapeDtypeStruct((WIRE, HD), BF16),
        ],
        in_specs=[vmem()] * (len(arrived) + 1) + [anywhere] * len(ready),
        out_specs=[vmem()] * 3,
        compiler_params=params(),
        name="sum_rows",
    )(*arrived.values(), bias, *ready)


def rotary_tables(shape_ref, counts_ref, tokens):
    place = lax.axis_index("seq")
    clip, member = lax.div(place, GROUP), lax.rem(place, GROUP)
    height, width = shape_ref[clip, 1], shape_ref[clip, 2]
    first_count = counts_ref[clip * GROUP]
    slot = lax.broadcasted_iota(jnp.int32, (GROUP * tokens, HD), 0)
    own = slot < tokens
    offset = jnp.where(own, member * first_count, (1 - member) * first_count - tokens)
    position = (slot + offset).astype(F32)

    def quotient(values, divisor):
        return jnp.floor((values + 0.5) / divisor.astype(F32))

    line = quotient(position, width)
    frame = quotient(position, height * width)
    row = line - frame * height.astype(F32)
    column = position - line * width.astype(F32)

    other_pairs = HD // 6
    frame_pairs = HD // 2 - 2 * other_pairs
    lane = lax.broadcasted_iota(jnp.int32, (1, HD), 1)
    pair = lax.rem(lane, HD // 2)
    in_frame = pair < frame_pairs
    in_row = pair < frame_pairs + other_pairs
    before = jnp.where(in_frame, 0, jnp.where(in_row, frame_pairs, frame_pairs + other_pairs))
    span = jnp.where(in_frame, 2.0 * frame_pairs, 2.0 * other_pairs)
    inverse = jnp.exp(-(2.0 * (pair - before).astype(F32) / span) * math.log(10000.0))
    angles = jnp.where(in_frame, frame, jnp.where(in_row, row, column)) * inverse
    return jnp.cos(angles), jnp.sin(angles) * jnp.where(lane < HD // 2, -1.0, 1.0)


def pairs_apart():
    source = lax.broadcasted_iota(jnp.int32, (HD, HD), 0)
    lane = lax.broadcasted_iota(jnp.int32, (HD, HD), 1)
    wanted = 2 * lax.rem(lane, HD // 2) + lax.div(lane, HD // 2)
    return jnp.where(source == wanted, 1.0, 0.0).astype(BF16)


def spread_kernel(
    shape_ref,
    counts_ref,
    mine_ref,
    other_ref,
    here_ref,
    there_ref,
    gain_ref,
    bias_q_ref,
    bias_kv_ref,
    ready_ref,
    left_ref,
    turned_ref,
    spread_ref,
    cosine_ref,
    sine_ref,
    gain_apart_ref,
    bias_ref,
):
    tokens = mine_ref.shape[0]
    query_cols, pair_cols = bias_q_ref.shape[1], bias_kv_ref.shape[1]
    place = 0
    for block in range(BLOCKS):
        for first, size in block_spans(block, (query_cols + pair_cols) // HD):
            for ref, low in ((bias_q_ref, 0), (bias_kv_ref, query_cols)):
                start, stop = max(first, low), min(first + size, low + ref.shape[1])
                if start < stop:
                    here = pl.ds(place + start - first, stop - start)
                    values = ref[:, pl.ds(start - low, stop - start)]
                    bias_ref[:, here] = jnp.broadcast_to(values, (8, stop - start))
            place += size
    apart = pairs_apart()
    for head in range(gain_ref.shape[1] // HD):
        own = pl.ds(head * HD, HD)
        for which in range(2):
            gain = jnp.broadcast_to(gain_ref[which : which + 1, own], (8, HD))
            gain_apart_ref[which, :, own] = sum(
                jnp.dot(piece, apart, preferred_element_type=F32)
                for piece in exact_pieces(gain, 3)
            )
    cosine_ref[...], sine_ref[...] = rotary_tables(shape_ref, counts_ref, tokens)
    for part, ref in enumerate((mine_ref, other_ref)):
        rows = ref[...]
        pieces = []
        for half_ref in (here_ref, there_ref):
            pieces.append(
                jnp.dot(rows, half_ref[0:64], preferred_element_type=F32) + bundle_bias(half_ref)
            )
        average = sum(jnp.sum(piece, axis=1, keepdims=True) for piece in pieces) * (1.0 / D)
        squares = sum(
            jnp.sum((piece - average) * (piece - average), axis=1, keepdims=True)
            for piece in pieces
        )
        spread = jnp.sqrt(squares * (1.0 / D) + EPSILON)
        spread = jnp.broadcast_to(spread, (tokens, HD))
        first = spread.astype(BF16).astype(F32)
        lane = lax.broadcasted_iota(jnp.int32, (tokens, HD), 1)
        extra = jnp.where(
            (lane == 64) | (lane == 66),
            1.0,
            jnp.where(
                (lane == 65) | (lane == 67), first, jnp.where(lane == 68, spread - first, 0.0)
            ),
        )
        patch = jnp.concatenate([rows.astype(F32), jnp.zeros((tokens, HD - 64), F32)], axis=1)
        left = jnp.where(lane < 64, patch, extra)
        here = pl.ds(part * tokens, tokens)
        left_ref[here] = left.astype(BF16)
        turned_ref[:, here] = left.T.astype(BF16)
        spread_ref[here] = spread


def spread_rows(clip_shape, shard_counts, mine, other, here, there, gains, biases, ready):
    tokens = mine.shape[0]
    return pl.pallas_call(
        spread_kernel,
        out_shape=[
            jax.ShapeDtypeStruct((2 * tokens, HD), BF16),
            jax.ShapeDtypeStruct((HD, 2 * tokens), BF16),
        ]
        + [jax.ShapeDtypeStruct((2 * tokens, HD), F32)] * 3
        + [jax.ShapeDtypeStruct((2, 8, gains.shape[1]), F32)]
        + [jax.ShapeDtypeStruct((8, BLOCKS * ready.shape[1]), F32)],
        in_specs=[smem()] * 2 + [vmem()] * 7 + [pl.BlockSpec(memory_space=pl.ANY)],
        out_specs=[vmem()] * 7,
        compiler_params=params(),
        name="spread_rows",
    )(clip_shape, shard_counts, mine, other, here, there, gains, *biases, ready)


def heads_kernel(
    heads_here,
    counts_ref,
    left_ref,
    mine_ref,
    theirs_ref,
    spread_ref,
    cosine_ref,
    sine_ref,
    gain_ref,
    q_ref,
    k_ref,
    v_ref,
    rows,
):
    tokens = q_ref.shape[0]
    whole, shared = block_chunks(3 * heads_here)
    lane = lax.broadcasted_iota(jnp.int32, (WIRE, HD), 1)
    for half in range(2):
        near = near_core(half)
        for ref, core in ((mine_ref, near), (theirs_ref, 1 - near)):
            for chunk in range(whole):
                columns = ref[half, :, chunk * HD : (chunk + 1) * HD]
                rows[(half * 2 + core) * whole + chunk, 0:WIRE] = columns
        last = pl.ds(whole * HD, HD)
        mine, theirs = mine_ref[half, :, last].astype(F32), theirs_ref[half, :, last].astype(F32)
        columns = jnp.where(free_lanes(lane, near), theirs, mine)
        rows[shared + half, 0:WIRE] = columns.astype(BF16)
    place = lax.axis_index("seq")
    count_own, count_other = counts_ref[place], counts_ref[jnp.bitwise_xor(place, 1)]
    slot = lax.broadcasted_iota(jnp.int32, (2 * tokens, HD), 0)
    valid = slot < jnp.where(slot < tokens, count_own, tokens + count_other)
    left = left_ref[:, 0:WIRE]
    inverse = jnp.where(valid, 1.0 / spread_ref[...], 0.0)
    turned = list(range(heads_here)) + [heads_here + 2 * head for head in range(heads_here)]
    together = jnp.concatenate([rows[chunk] for chunk in turned], axis=0)
    together = jnp.dot(together, pairs_apart(), preferred_element_type=F32).astype(BF16)

    def projected(first, second, count):
        weight = jnp.concatenate([first, second], axis=1)
        found = jnp.dot(left[:count], weight, preferred_element_type=F32)
        return found[:, :HD], found[:, HD:]

    def rotated(values, gain, count):
        values = values * gain
        return values * cosine_ref[:count] + pltpu.roll(values, HD // 2, 1) * sine_ref[:count]

    def apart(index):
        return together[index * STEP : index * STEP + WIRE]

    for head in range(0, heads_here, 2):
        pair = (head, head + 1)
        for turn, found in zip(pair, projected(*[apart(turn) for turn in pair], tokens)):
            own = pl.ds(turn * HD, HD)
            q_ref[:, own] = rotated(found, gain_ref[0, 0:1, own], tokens)
        weights = [apart(heads_here + turn) for turn in pair]
        for turn, found in zip(pair, projected(*weights, 2 * tokens)):
            own = pl.ds(turn * HD, HD)
            k_ref[:, own] = rotated(found, gain_ref[1, 0:1, own], 2 * tokens).astype(BF16)
        weights = [rows[heads_here + 2 * turn + 1, 0:WIRE] for turn in pair]
        for turn, found in zip(pair, projected(*weights, 2 * tokens)):
            v_ref[:, pl.ds(turn * HD, HD)] = (found * inverse).astype(BF16)


def heads_rows(counts, left, mine, theirs, spread, cosine, sine, gains, heads_here):
    both = left.shape[0]
    wide = heads_here * HD
    return pl.pallas_call(
        functools.partial(heads_kernel, heads_here),
        out_shape=[
            jax.ShapeDtypeStruct((both // 2, wide), F32),
            jax.ShapeDtypeStruct((both, wide), BF16),
            jax.ShapeDtypeStruct((both, wide), BF16),
        ],
        in_specs=[smem()] + [vmem()] * 7,
        out_specs=[vmem()] * 3,
        scratch_shapes=[pltpu.VMEM((3 * heads_here, STEP, HD), BF16)],
        compiler_params=params(),
        name="heads_rows",
    )(counts, left, mine, theirs, spread, cosine, sine, gains)


def attend_kernel(
    heads_here, counts_ref, q_ref, k_ref, v_ref, left_ref, turned_ref, theirs_ref, *refs
):
    gram_refs, (out_ref, found, sems) = refs[:-3], refs[-3:]
    tokens = q_ref.shape[0]
    place = lax.axis_index("seq")
    count_own, count_other = counts_ref[place], counts_ref[jnp.bitwise_xor(place, 1)]

    left = left_ref[0:tokens, 0:WIRE]
    turned = turned_ref[0:WIRE]
    last = theirs_ref.shape[2] - HD
    gram = sum(ref[...].astype(F32) for ref in gram_refs)
    for place in range(2):
        gram = gram + theirs_ref[place, :, last:].astype(F32)
    gram = gram * (1.0 / D)
    gram_q, gram_k = [exact_pieces(values, 2) for values in gram_halves(gram)]
    spun_q = sum(jnp.dot(left, piece, preferred_element_type=F32) for piece in gram_q)
    wide_left = left_ref[0:tokens].astype(F32)
    square_q = jnp.sum(spun_q * wide_left[:, 0:WIRE], axis=1, keepdims=True)
    spread_q = wide_left[:, 65:66] + wide_left[:, 68:69]
    scale_q = lax.rsqrt(square_q + EPSILON * spread_q * spread_q) * (
        math.log2(math.e) / math.sqrt(HD)
    )
    scale_q = jnp.broadcast_to(scale_q, (tokens, HD))
    spun_k = sum(jnp.dot(piece, turned, preferred_element_type=F32) for piece in gram_k)
    wide_turned = turned.astype(F32)
    square_k = jnp.sum(spun_k * wide_turned, axis=0, keepdims=True)
    spread_k = wide_turned[65:66] + wide_turned[68:69]
    scale_k = lax.rsqrt(square_k + EPSILON * spread_k * spread_k)
    slot = lax.broadcasted_iota(jnp.int32, (1, 2 * tokens), 1)
    valid = slot < jnp.where(slot < tokens, count_own, tokens + count_other)
    scale_k = jnp.where(valid, scale_k, 0.0)

    slot = lax.broadcasted_iota(jnp.int32, (2 * tokens, HD), 0)
    valid = slot < jnp.where(slot < tokens, count_own, tokens + count_other)
    ones = jnp.where(valid, 1.0, 0.0).astype(BF16)
    row = lax.broadcasted_iota(jnp.int32, (tokens, HD), 0)
    contract = (((1,), (1,)), ((), ()))

    def scores_of(head):
        own = pl.ds(head * HD, HD)
        query = (q_ref[:, own] * scale_q).astype(BF16)
        return lax.dot_general(query, k_ref[:, own], contract, preferred_element_type=F32)

    copies = []
    scores = scores_of(0)
    for head in range(heads_here):
        own = pl.ds(head * HD, HD)
        later = scores_of(head + 1) if head + 1 < heads_here else None
        weights = jnp.exp2(scores * scale_k).astype(BF16)
        values = jnp.concatenate([v_ref[:, own], ones], axis=1)
        result = jnp.dot(weights, values, preferred_element_type=F32)
        result = result[:, 0:HD] / result[:, HD:]
        found[:, own] = jnp.where(row < count_own, result, 0.0).astype(BF16)
        copies.append(pltpu.make_async_copy(found.at[:, own], out_ref.at[:, own], sems.at[head]))
        copies[-1].start()
        scores = later
    for copy in copies:
        copy.wait()


def attend_rows(counts, queries, keys, values, left, turned, theirs, grams):
    heads_here = queries.shape[1] // HD
    return pl.pallas_call(
        functools.partial(attend_kernel, heads_here),
        out_shape=jax.ShapeDtypeStruct(queries.shape, BF16),
        in_specs=[smem()] + [vmem()] * (6 + len(grams)),
        out_specs=pl.BlockSpec(memory_space=pl.ANY),
        scratch_shapes=[
            pltpu.VMEM(queries.shape, BF16),
            pltpu.SemaphoreType.DMA((heads_here,)),
        ],
        compiler_params=params(),
        name="attend_rows",
    )(counts, queries, keys, values, left, turned, theirs, *grams)


def shards(
    patches,
    clip_shape,
    shard_counts,
    patch_weight,
    patch_bias,
    time_mod,
    block_mod,
    w_query,
    query_bias,
    w_keyvalue,
    keyvalue_bias,
    norm_gain,
):
    tokens = patches.shape[0]
    heads_here = w_query.shape[1] // HD
    count = lax.axis_size("seq")
    halves = lax.axis_size("mp")
    place = lax.axis_index("seq")
    clips = time_mod.shape[0]
    rows = w_query.shape[0]
    padded = -(-rows // 16) * 16
    clips_sent = count // 4

    def pad_rows(values):
        return values if rows == padded else jnp.pad(values, ((0, padded - rows), (0, 0)))

    packed = pack_weights(pad_rows(w_query), pad_rows(w_keyvalue))
    pieces = [packed[0]] + [swap_bits(packed[flip], 2 * flip) for flip in range(1, BLOCKS)]
    first_swapped = swap_bits(packed[0], 1)

    features = patch_bias.shape[0]
    own, own_patches = prepare_rows(
        patch_weight, patch_bias[None], time_mod, block_mod, patches, first_swapped
    )
    other = lax.ppermute(own, "mp", [(i, (i + 1) % halves) for i in range(halves)])
    other_patches = swap_bits(own_patches, 1)
    span = 8 * rows

    def group_part(values):
        if span == features and rows == padded:
            return values
        values = lax.dynamic_slice_in_dim(values, place // 8 * span % features, span, 1)
        values = jnp.pad(
            values.reshape(-1, 8, rows), ((0, 0), (0, 0), (0, padded - rows))
        )
        return values.reshape(-1, 8 * padded)

    rows_here, rest_here = modulated_rows(
        own, other, group_part(own), group_part(other), clips_sent, span
    )
    placed = {0: packed[0], 1: first_swapped}
    for flip in reversed(range(1, BLOCKS)):
        piece = after(pieces[flip], rows_here, other_patches)
        placed[2 * flip], placed[2 * flip + 1] = piece, swap_bits(piece, 1)
    first = {order: placed.pop(order) for order in (6, 4, 5, 2, 3, 0, 1)}
    early = early_rows(rows_here, rest_here, first, padded)

    products = product_rows(rows_here, rest_here, early, placed, clips_sent, padded)
    arrived = {}
    for flip in reversed(range(clips_sent)):
        pairs = []
        for source in range(count):
            rest, second, core = source // 4, source // 2 % 2, source % 2
            turn = flip % 2
            pairs.append((source, (rest ^ flip) * 4 + (core ^ turn) * 2 + (second ^ turn)))
        arrived[flip] = lax.ppermute(products[flip], "seq", pairs)
    biases = (query_bias[None], keyvalue_bias[None])
    left, turned, spread, cosine, sine, gains, bias = spread_rows(
        clip_shape,
        shard_counts,
        own_patches,
        other_patches,
        own,
        other,
        norm_gain,
        biases,
        products[0],
    )

    mine, gram, gram_sent = sum_rows(arrived, bias, w_query.shape[1], w_keyvalue.shape[1], (left,))
    theirs = swap_bits(mine, 1)
    far_mp = [(i, (i + 1) % halves) for i in range(halves)]
    far_both = [
        (core * halves + i, (core ^ 1) * halves + j) for core in range(count) for i, j in far_mp
    ]
    grams = (
        gram,
        lax.ppermute(gram_sent, "mp", far_mp),
        lax.ppermute(gram_sent, ("seq", "mp"), far_both),
    )
    queries, keys, values = heads_rows(
        shard_counts, left, mine, theirs, spread, cosine, sine, gains, heads_here
    )
    return attend_rows(shard_counts, queries, keys, values, left, turned, theirs, grams)


def solution(mesh):
    return jax.shard_map(
        shards,
        mesh=mesh,
        in_specs=(
            P("seq", None),
            P(),
            P(),
            P(None, "mp"),
            P("mp"),
            P(None, None, "mp"),
            P(None, "mp"),
            P("seq", "mp"),
            P("mp"),
            P("seq", "mp"),
            P("mp"),
            P(None, "mp"),
        ),
        out_specs=P("seq", "mp"),
        check_vma=False,
    )
```

```python
import functools
import math

import jax
import jax.numpy as jnp
from jax import lax
from jax.experimental import pallas as pl
from jax.experimental.pallas import tpu as pltpu
from jax.sharding import PartitionSpec as P

D = 2560
HEADS = 20
HD = 128
GROUP = 2
EPSILON = 1e-06

BLOCKS = 4
WIRE = 72
STEP = 80
VMEM_LIMIT = 24 * 1024 * 1024
F32 = jnp.float32
BF16 = jnp.bfloat16


def params():
    return pltpu.CompilerParams(vmem_limit_bytes=VMEM_LIMIT)


def vmem():
    return pl.BlockSpec(memory_space=pltpu.VMEM)


def smem():
    return pl.BlockSpec(memory_space=pltpu.SMEM)


def swap_bits(value, mask):
    count = lax.axis_size("seq")
    return lax.ppermute(value, "seq", [(source, source ^ mask) for source in range(count)])


def exact_pieces(values, pieces):
    found = []
    for _ in range(pieces):
        piece = values.astype(BF16)
        found.append(piece)
        values = values - piece.astype(F32)
    return found


def block_chunks(chunks):
    whole = chunks // BLOCKS
    assert chunks - BLOCKS * whole == BLOCKS // 2
    return whole, BLOCKS * whole


def block_spans(block, chunks):
    whole, shared = block_chunks(chunks)
    return (block * whole * HD, whole * HD), ((shared + block // 2) * HD, HD)


def chip_block():
    return lax.rem(lax.div(lax.axis_index("seq"), 2), BLOCKS)


def after(value, *ready):
    anywhere = pl.BlockSpec(memory_space=pl.ANY)
    return pl.pallas_call(
        lambda *refs: None,
        out_shape=jax.ShapeDtypeStruct(value.shape, value.dtype),
        in_specs=[anywhere] * (1 + len(ready)),
        out_specs=anywhere,
        input_output_aliases={0: 0},
        compiler_params=pltpu.CompilerParams(vmem_limit_bytes=1024 * 1024),
        name="after",
    )(value, *ready)


def prepare_kernel(
    weight_ref, bias_ref, time_ref, block_ref, patches_ref, ready_ref, bundle_ref, copy_ref, mods
):
    clips = time_ref.shape[0]
    bundle_ref[0:64] = weight_ref[...]
    row = lax.broadcasted_iota(jnp.int32, (16, bundle_ref.shape[1]), 0)
    pieces = exact_pieces(bias_ref[...], 3)
    bundle_ref[64:80] = sum(
        jnp.where(row == which, piece.astype(F32), 0.0) for which, piece in enumerate(pieces)
    ).astype(BF16)
    for clip in range(clips):
        mods[pl.ds(2 * clip, 2)] = time_ref[clip] + block_ref[...]
    for which, piece in enumerate(exact_pieces(mods[...], 2)):
        bundle_ref[pl.ds(80 + 2 * clips * which, 2 * clips)] = piece
    copy_ref[...] = patches_ref[...]


def prepare_rows(weight, bias, time_mod, block_mod, patches, ready):
    clips, _, features = time_mod.shape
    return pl.pallas_call(
        prepare_kernel,
        out_shape=[
            jax.ShapeDtypeStruct((80 + 4 * clips, features), BF16),
            jax.ShapeDtypeStruct(patches.shape, BF16),
        ],
        in_specs=[vmem()] * 5 + [pl.BlockSpec(memory_space=pl.ANY)],
        out_specs=[vmem()] * 2,
        scratch_shapes=[pltpu.VMEM((2 * clips, features), F32)],
        compiler_params=params(),
        name="prepare_rows",
    )(weight, bias, time_mod, block_mod, patches, ready)


def bundle_bias(ref):
    return jnp.sum(ref[64:80].astype(F32), axis=0, keepdims=True)


def pack_kernel(wq_ref, wkv_ref, *refs):
    out_refs, (shared, sems, shared_sem) = refs[:-3], refs[-3:]
    rows, query_cols = wq_ref.shape
    chunks = (query_cols + wkv_ref.shape[1]) // HD
    whole, first_shared = block_chunks(chunks)
    mine = chip_block()

    def chunk_of(chunk):
        if chunk * HD < query_cols:
            return wq_ref.at[:, pl.ds(chunk * HD, HD)]
        return wkv_ref.at[:, pl.ds(chunk * HD - query_cols, HD)]

    copies = [
        pltpu.make_async_copy(chunk_of(first_shared + which), shared.at[which], shared_sem.at[which])
        for which in range(BLOCKS // 2)
    ]
    for copy in copies:
        copy.start()
    for flip in range(1, BLOCKS + 1):
        flip = flip % BLOCKS
        for block in range(BLOCKS):

            @pl.when(jnp.bitwise_xor(mine, flip) == block)
            def _(flip=flip, block=block):
                for chunk in range(whole):
                    pltpu.make_async_copy(
                        chunk_of(block * whole + chunk),
                        out_refs[flip].at[pl.ds(chunk * rows, rows)],
                        sems.at[flip],
                    ).start()

    for copy in copies:
        copy.wait()
    lane = lax.broadcasted_iota(jnp.int32, (rows // 2, HD), 1)
    for flip in range(BLOCKS):
        block = jnp.bitwise_xor(mine, flip)
        values = shared[lax.div(block, 2)].astype(F32)
        above, below = values[: rows // 2], values[rows // 2 :]
        even = jnp.where(lane < HD // 2, above, pltpu.roll(below, HD // 2, 1))
        odd = jnp.where(lane < HD // 2, pltpu.roll(above, HD // 2, 1), below)
        found = jnp.where(lax.rem(block, 2) == 0, even, odd)
        out_refs[flip][pl.ds(whole * rows, rows // 2)] = found.astype(BF16)
    for flip in range(BLOCKS):
        here = out_refs[flip].at[pl.ds(0, whole * rows)]
        pltpu.make_async_copy(here, here, sems.at[flip]).wait()


def pack_weights(w_query, w_keyvalue):
    rows = w_query.shape[0]
    whole, _ = block_chunks((w_query.shape[1] + w_keyvalue.shape[1]) // HD)
    return pl.pallas_call(
        pack_kernel,
        out_shape=[jax.ShapeDtypeStruct((whole * rows + rows // 2, HD), BF16)] * BLOCKS,
        in_specs=[pl.BlockSpec(memory_space=pltpu.HBM)] * 2,
        out_specs=[vmem()] * BLOCKS,
        scratch_shapes=[
            pltpu.VMEM((BLOCKS // 2, rows, HD), BF16),
            pltpu.SemaphoreType.DMA((BLOCKS,)),
            pltpu.SemaphoreType.DMA((BLOCKS // 2,)),
        ],
        compiler_params=params(),
        name="pack_weights",
    )(*[pltpu.with_memory_space_constraint(w, pltpu.HBM) for w in (w_query, w_keyvalue)])


def reorder_blocks(values, low):
    for bit in (2, 1, 0):
        count = 8 >> bit
        size = values.shape[1] // count
        blocks = [values[:, j * size : (j + 1) * size] for j in range(count)]
        swapped = jnp.concatenate([blocks[j ^ 1] for j in range(count)], axis=1)
        values = jnp.where(jnp.bitwise_and(low, 1 << bit) != 0, swapped, values)
    return values


def modulated_kernel(
    clips_sent, span, own_ref, other_ref, own_part_ref, other_part_ref, rows_ref, part
):
    place = lax.axis_index("seq")
    rest, core = lax.div(place, 4), lax.rem(place, 2)
    mods_rows = (own_ref.shape[0] - 80) // 2
    total = jnp.sum(own_ref[0:64].astype(F32), axis=1, keepdims=True)
    total = total + jnp.sum(other_ref[0:64].astype(F32), axis=1, keepdims=True)
    total_bias = jnp.sum(bundle_bias(own_ref) + bundle_bias(other_ref), axis=1, keepdims=True)
    owner = lax.div(lax.div(place, 8) * span, own_ref.shape[1])

    def unbundled(ref):
        mods = ref[80 : 80 + mods_rows].astype(F32) + ref[80 + mods_rows :].astype(F32)
        bias = jnp.broadcast_to(bundle_bias(ref), (8, mods.shape[1]))
        return jnp.concatenate([ref[0:64].astype(F32), bias, mods], axis=0)

    @pl.when(owner == lax.axis_index("mp"))
    def _():
        part[...] = unbundled(own_part_ref)

    @pl.when(owner != lax.axis_index("mp"))
    def _():
        part[...] = unbundled(other_part_ref)

    part[...] = reorder_blocks(part[...], jnp.bitwise_and(place, 7))
    centred = part[0:64] - total * (1.0 / D)
    centred_bias = part[64:65] - total_bias * (1.0 / D)
    row = lax.broadcasted_iota(jnp.int32, (STEP - 64, centred.shape[1]), 0)
    for flip in range(clips_sent):
        clip = jnp.bitwise_xor(rest, flip) * 2 + jnp.bitwise_xor(core, flip % 2)
        eight = part[pl.ds(pl.multiple_of(72 + 8 * lax.div(clip, 4), 8), 8)]
        first = 2 * lax.rem(clip, 4)
        shift = jnp.sum(jnp.where(row[:8] == first, eight, 0.0), axis=0, keepdims=True)
        scale = 1.0 + jnp.sum(jnp.where(row[:8] == first + 1, eight, 0.0), axis=0, keepdims=True)
        patch_rows = centred * scale
        extra = jnp.where(row == 0, centred_bias * scale, jnp.where(row == 1, shift, 0.0))
        rows_ref[pl.ds(flip * STEP, 64)] = patch_rows.astype(BF16)
        rows_ref[pl.ds(flip * STEP + 64, STEP - 64)] = extra.astype(BF16)


def modulated_rows(own, other, own_part, other_part, clips_sent, span):
    return pl.pallas_call(
        functools.partial(modulated_kernel, clips_sent, span),
        out_shape=jax.ShapeDtypeStruct((clips_sent * STEP, own_part.shape[1]), BF16),
        in_specs=[vmem()] * 4,
        out_specs=vmem(),
        scratch_shapes=[pltpu.VMEM((72 + (own.shape[0] - 80) // 2, own_part.shape[1]), F32)],
        compiler_params=params(),
        name="modulated_rows",
    )(own, other, own_part, other_part)


def free_lanes(lane, odd):
    return jnp.where(odd == 1, 0, HD // 2) == HD // 2 * lax.div(lane, HD // 2)


def doubled(values, lane, second):
    turned = pltpu.roll(values, HD // 2, 1)
    return jnp.where((lane < HD // 2) == (not second), values, turned)


def piece_chunks(refs, rows):
    whole = refs[0].shape[0] // rows
    for chunk in range(whole):
        yield jnp.concatenate([ref[pl.ds(chunk * rows, rows)] for ref in refs], axis=0)
    parts = []
    for ref in refs:
        half = ref[pl.ds(whole * rows, rows // 2)]
        parts += [half, pltpu.roll(half.astype(F32), HD // 2, 1).astype(BF16)]
    yield jnp.concatenate(parts, axis=0)


def piece_products(rows_here, refs, rows):
    chunks = list(piece_chunks(refs, rows))
    for chunk in range(0, len(chunks), 2):
        block = jnp.concatenate(chunks[chunk : chunk + 2], axis=1)
        yield chunk, jnp.dot(rows_here, block, preferred_element_type=F32)


def early_kernel(order, rows, rows_ref, *refs):
    out_ref = refs[-1]
    refs = [refs[order.index(block)] for block in sorted(order)]
    for chunk, total in piece_products(rows_ref[:, 0 : len(refs) * rows], refs, rows):
        out_ref[:, pl.ds(chunk * HD, 2 * HD)] = total


def early_rows(rows_here, pieces, rows):
    wide = (pieces[0].shape[0] // rows + 1) * HD
    return pl.pallas_call(
        functools.partial(early_kernel, list(pieces), rows),
        out_shape=jax.ShapeDtypeStruct((rows_here.shape[0], wide), F32),
        in_specs=[vmem()] * (1 + len(pieces)),
        out_specs=vmem(),
        compiler_params=params(),
        name="early_rows",
    )(rows_here, *pieces.values())


def product_kernel(clips_sent, order, rows, rows_ref, early_ref, *refs):
    refs, out_refs = refs[: len(order)], refs[len(order) :]
    refs = [refs[order.index(block)] for block in sorted(order)]
    done = rows_ref.shape[1] - len(order) * rows
    wide = early_ref.shape[1]
    tile = 2 * HD
    lane = lax.broadcasted_iota(jnp.int32, (8, HD), 1)
    row = lax.broadcasted_iota(jnp.int32, (8, HD), 0)
    odd = lax.rem(chip_block(), 2)
    ends = [[] for _ in range(clips_sent)]
    for first_chunk, total in piece_products(rows_ref[:, done:], refs, rows):
        start = first_chunk * HD
        columns = pl.ds(start, tile)
        total = total + early_ref[:, columns]
        for flip in range(clips_sent):
            base = flip * STEP
            for chunk in range(0, tile, HD):
                end = total[base + 64 : base + 72, chunk : chunk + HD]
                first = end.astype(BF16).astype(F32)
                end = first + pltpu.roll(end - first, 2, 0)
                low = doubled(end, lane, False)
                high = low if start + chunk + HD == wide else doubled(end, lane, True)
                ends[flip].append(jnp.where(row < 4, low, pltpu.roll(high, 4, 0)))
            patch_rows = total[base : base + 64]
            if start + tile == wide:
                wide_lane = lax.broadcasted_iota(jnp.int32, (64, HD), 1)
                last = jnp.where(
                    free_lanes(wide_lane, odd),
                    jnp.concatenate(ends[flip], axis=0),
                    doubled(patch_rows[:, tile - HD :], wide_lane, False),
                )
                patch_rows = jnp.concatenate([patch_rows[:, : tile - HD], last], axis=1)
            out_refs[flip][:, columns] = patch_rows.astype(BF16)


def product_rows(rows_here, early, pieces, clips_sent, rows):
    return pl.pallas_call(
        functools.partial(product_kernel, clips_sent, list(pieces), rows),
        out_shape=[jax.ShapeDtypeStruct((64, early.shape[1]), BF16)] * clips_sent,
        in_specs=[vmem()] * (2 + len(pieces)),
        out_specs=[vmem()] * clips_sent,
        compiler_params=params(),
        name="product_rows",
    )(rows_here, early, *pieces.values())


def split_ends(ends, row):
    ends = jnp.where(row < 2, ends + pltpu.roll(ends, 6, 0), 0.0)
    first = ends.astype(BF16).astype(F32)
    return first + pltpu.roll(ends - first, 2, 0)


def near_core(half):
    place = lax.axis_index("seq")
    core, low = lax.rem(place, 2), lax.rem(lax.div(place, 4), 2)
    return jnp.bitwise_xor(core, jnp.bitwise_xor(low, half))


def sum_kernel(flips, query_cols, pair_cols, *refs):
    in_refs, bias_ref = refs[: len(flips)], refs[len(flips)]
    out_ref, gram_ref, gram_sent_ref = refs[-3:]
    wide = out_ref.shape[2] - HD
    chunks = wide // HD
    own = lax.rem(lax.div(lax.axis_index("seq"), 4), 2)
    row = lax.broadcasted_iota(jnp.int32, (8, wide), 0)
    lane = lax.broadcasted_iota(jnp.int32, (1, wide), 1)
    chunk_lane = lax.broadcasted_iota(jnp.int32, (64, HD), 1)
    contract = (((1,), (1,)), ((), ()))
    grams = [jnp.zeros((WIRE, WIRE), F32)] * 2
    for parity in range(2):
        half = jnp.bitwise_xor(own, parity)
        odd = near_core(half)
        total = sum(ref[...].astype(F32) for ref, flip in zip(in_refs, flips) if flip % 2 == parity)
        last = total[:, wide - HD :]
        free = free_lanes(chunk_lane, odd)
        kept = jnp.where(free, last, pltpu.roll(last, HD // 2, 1))
        ends = []
        for chunk in range(chunks):
            eight = kept[8 * chunk : 8 * chunk + 8]
            ends.append(jnp.where(chunk_lane[:8] < HD // 2, eight, pltpu.roll(eight, 4, 0)))
        ends[-1] = kept[64 - 8 :]
        ends = jnp.where(row < 4, jnp.concatenate(ends, axis=1), 0.0)
        first = pl.multiple_of((half * 2 + odd) * wide, HD)
        ends = ends + jnp.where(row == 1, bias_ref[:, pl.ds(first, wide)], 0.0)
        ends = split_ends(ends, row)
        ends = ends + jnp.where(row == 4, pltpu.roll(ends, 3, 0), 0.0)
        rows = jnp.concatenate([total, ends], axis=0).astype(BF16)
        out_ref[half, :, 0:wide] = rows
        column = lane + (half * 2 + odd) * (wide - HD)
        tail = lane - (wide - HD)
        in_tail = tail >= 0
        column = jnp.where(in_tail, tail + BLOCKS * (wide - HD) + half * HD, column)
        held = jnp.logical_or(lane < wide - HD, lax.div(tail, HD // 2) == odd)
        pair = column - query_cols
        is_key = (pair >= 0) & (lax.rem(pair, 2 * HD) < HD)
        for which, keep in enumerate((pair < 0, is_key)):
            keep = jnp.where(keep, 1.0, 0.0) * jnp.where(held, 1.0, 0.0)
            kept = jnp.where(keep > 0.0, rows.astype(F32), 0.0).astype(BF16)
            grams[which] += lax.dot_general(kept, kept, contract, preferred_element_type=F32)
    row = lax.broadcasted_iota(jnp.int32, (WIRE, WIRE), 0)
    column = lax.broadcasted_iota(jnp.int32, (WIRE, WIRE), 1)
    both = jnp.where(
        row < column, 2.0 * grams[0], jnp.where(row == column, grams[0], 2.0 * grams[1])
    )
    diagonal = jnp.sum(jnp.where(row == column, grams[1], 0.0), axis=1, keepdims=True)
    gram_ref[:, 0:WIRE] = both
    gram_ref[:, WIRE:] = jnp.broadcast_to(diagonal, (WIRE, HD - WIRE))
    gram_sent_ref[...] = gram_ref[...].astype(BF16)
    for place, piece in enumerate(exact_pieces(gram_ref[...], 2)):
        out_ref[place, :, pl.ds(wide, HD)] = piece


def gram_halves(gram):
    row = lax.broadcasted_iota(jnp.int32, (WIRE, WIRE), 0)
    column = lax.broadcasted_iota(jnp.int32, (WIRE, WIRE), 1)
    both = gram[:, 0:WIRE]
    queries = jnp.where(row <= column, both, 0.0)
    keys = jnp.where(row > column, both, jnp.where(row == column, gram[:, WIRE : WIRE + 1], 0.0))
    return queries, keys


def sum_rows(arrived, bias, query_cols, pair_cols, ready):
    wide = next(iter(arrived.values())).shape[1]
    anywhere = pl.BlockSpec(memory_space=pl.ANY)
    return pl.pallas_call(
        functools.partial(sum_kernel, list(arrived), query_cols, pair_cols),
        out_shape=[
            jax.ShapeDtypeStruct((2, WIRE, wide + HD), BF16),
            jax.ShapeDtypeStruct((WIRE, HD), F32),
            jax.ShapeDtypeStruct((WIRE, HD), BF16),
        ],
        in_specs=[vmem()] * (len(arrived) + 1) + [anywhere] * len(ready),
        out_specs=[vmem()] * 3,
        compiler_params=params(),
        name="sum_rows",
    )(*arrived.values(), bias, *ready)


def rotary_tables(shape_ref, counts_ref, tokens):
    place = lax.axis_index("seq")
    clip, member = lax.div(place, GROUP), lax.rem(place, GROUP)
    height, width = shape_ref[clip, 1], shape_ref[clip, 2]
    first_count = counts_ref[clip * GROUP]
    slot = lax.broadcasted_iota(jnp.int32, (GROUP * tokens, HD), 0)
    own = slot < tokens
    offset = jnp.where(own, member * first_count, (1 - member) * first_count - tokens)
    position = (slot + offset).astype(F32)

    def quotient(values, divisor):
        return jnp.floor((values + 0.5) / divisor.astype(F32))

    line = quotient(position, width)
    frame = quotient(position, height * width)
    row = line - frame * height.astype(F32)
    column = position - line * width.astype(F32)

    other_pairs = HD // 6
    frame_pairs = HD // 2 - 2 * other_pairs
    lane = lax.broadcasted_iota(jnp.int32, (1, HD), 1)
    pair = lax.rem(lane, HD // 2)
    in_frame = pair < frame_pairs
    in_row = pair < frame_pairs + other_pairs
    before = jnp.where(in_frame, 0, jnp.where(in_row, frame_pairs, frame_pairs + other_pairs))
    span = jnp.where(in_frame, 2.0 * frame_pairs, 2.0 * other_pairs)
    inverse = jnp.exp(-(2.0 * (pair - before).astype(F32) / span) * math.log(10000.0))
    angles = jnp.where(in_frame, frame, jnp.where(in_row, row, column)) * inverse
    return jnp.cos(angles), jnp.sin(angles) * jnp.where(lane < HD // 2, -1.0, 1.0)


def pairs_apart():
    source = lax.broadcasted_iota(jnp.int32, (HD, HD), 0)
    lane = lax.broadcasted_iota(jnp.int32, (HD, HD), 1)
    wanted = 2 * lax.rem(lane, HD // 2) + lax.div(lane, HD // 2)
    return jnp.where(source == wanted, 1.0, 0.0).astype(BF16)


def spread_kernel(
    shape_ref,
    counts_ref,
    mine_ref,
    other_ref,
    here_ref,
    there_ref,
    gain_ref,
    bias_q_ref,
    bias_kv_ref,
    ready_ref,
    left_ref,
    turned_ref,
    spread_ref,
    cosine_ref,
    sine_ref,
    gain_apart_ref,
    bias_ref,
):
    tokens = mine_ref.shape[0]
    query_cols, pair_cols = bias_q_ref.shape[1], bias_kv_ref.shape[1]
    place = 0
    for block in range(BLOCKS):
        for first, size in block_spans(block, (query_cols + pair_cols) // HD):
            for ref, low in ((bias_q_ref, 0), (bias_kv_ref, query_cols)):
                start, stop = max(first, low), min(first + size, low + ref.shape[1])
                if start < stop:
                    here = pl.ds(place + start - first, stop - start)
                    values = ref[:, pl.ds(start - low, stop - start)]
                    bias_ref[:, here] = jnp.broadcast_to(values, (8, stop - start))
            place += size
    apart = pairs_apart()
    for head in range(gain_ref.shape[1] // HD):
        own = pl.ds(head * HD, HD)
        for which in range(2):
            gain = jnp.broadcast_to(gain_ref[which : which + 1, own], (8, HD))
            gain_apart_ref[which, :, own] = sum(
                jnp.dot(piece, apart, preferred_element_type=F32)
                for piece in exact_pieces(gain, 3)
            )
    cosine_ref[...], sine_ref[...] = rotary_tables(shape_ref, counts_ref, tokens)
    for part, ref in enumerate((mine_ref, other_ref)):
        rows = ref[...]
        pieces = []
        for half_ref in (here_ref, there_ref):
            pieces.append(
                jnp.dot(rows, half_ref[0:64], preferred_element_type=F32) + bundle_bias(half_ref)
            )
        average = sum(jnp.sum(piece, axis=1, keepdims=True) for piece in pieces) * (1.0 / D)
        squares = sum(
            jnp.sum((piece - average) * (piece - average), axis=1, keepdims=True)
            for piece in pieces
        )
        spread = jnp.sqrt(squares * (1.0 / D) + EPSILON)
        spread = jnp.broadcast_to(spread, (tokens, HD))
        first = spread.astype(BF16).astype(F32)
        lane = lax.broadcasted_iota(jnp.int32, (tokens, HD), 1)
        extra = jnp.where(
            (lane == 64) | (lane == 66),
            1.0,
            jnp.where(
                (lane == 65) | (lane == 67), first, jnp.where(lane == 68, spread - first, 0.0)
            ),
        )
        patch = jnp.concatenate([rows.astype(F32), jnp.zeros((tokens, HD - 64), F32)], axis=1)
        left = jnp.where(lane < 64, patch, extra)
        here = pl.ds(part * tokens, tokens)
        left_ref[here] = left.astype(BF16)
        turned_ref[:, here] = left.T.astype(BF16)
        spread_ref[here] = spread


def spread_rows(clip_shape, shard_counts, mine, other, here, there, gains, biases, ready):
    tokens = mine.shape[0]
    return pl.pallas_call(
        spread_kernel,
        out_shape=[
            jax.ShapeDtypeStruct((2 * tokens, HD), BF16),
            jax.ShapeDtypeStruct((HD, 2 * tokens), BF16),
        ]
        + [jax.ShapeDtypeStruct((2 * tokens, HD), F32)] * 3
        + [jax.ShapeDtypeStruct((2, 8, gains.shape[1]), F32)]
        + [jax.ShapeDtypeStruct((8, BLOCKS * ready.shape[1]), F32)],
        in_specs=[smem()] * 2 + [vmem()] * 7 + [pl.BlockSpec(memory_space=pl.ANY)],
        out_specs=[vmem()] * 7,
        compiler_params=params(),
        name="spread_rows",
    )(clip_shape, shard_counts, mine, other, here, there, gains, *biases, ready)


def heads_kernel(
    heads_here,
    counts_ref,
    left_ref,
    mine_ref,
    theirs_ref,
    spread_ref,
    cosine_ref,
    sine_ref,
    gain_ref,
    q_ref,
    k_ref,
    v_ref,
    rows,
):
    tokens = q_ref.shape[0]
    whole, shared = block_chunks(3 * heads_here)
    lane = lax.broadcasted_iota(jnp.int32, (WIRE, HD), 1)
    for half in range(2):
        near = near_core(half)
        for ref, core in ((mine_ref, near), (theirs_ref, 1 - near)):
            for chunk in range(whole):
                columns = ref[half, :, chunk * HD : (chunk + 1) * HD]
                rows[(half * 2 + core) * whole + chunk, 0:WIRE] = columns
        last = pl.ds(whole * HD, HD)
        mine, theirs = mine_ref[half, :, last].astype(F32), theirs_ref[half, :, last].astype(F32)
        columns = jnp.where(free_lanes(lane, near), theirs, mine)
        rows[shared + half, 0:WIRE] = columns.astype(BF16)
    place = lax.axis_index("seq")
    count_own, count_other = counts_ref[place], counts_ref[jnp.bitwise_xor(place, 1)]
    slot = lax.broadcasted_iota(jnp.int32, (2 * tokens, HD), 0)
    valid = slot < jnp.where(slot < tokens, count_own, tokens + count_other)
    left = left_ref[:, 0:WIRE]
    inverse = jnp.where(valid, 1.0 / spread_ref[...], 0.0)
    turned = list(range(heads_here)) + [heads_here + 2 * head for head in range(heads_here)]
    together = jnp.concatenate([rows[chunk] for chunk in turned], axis=0)
    together = jnp.dot(together, pairs_apart(), preferred_element_type=F32).astype(BF16)

    def projected(first, second, count):
        weight = jnp.concatenate([first, second], axis=1)
        found = jnp.dot(left[:count], weight, preferred_element_type=F32)
        return found[:, :HD], found[:, HD:]

    def rotated(values, gain, count):
        values = values * gain
        return values * cosine_ref[:count] + pltpu.roll(values, HD // 2, 1) * sine_ref[:count]

    def apart(index):
        return together[index * STEP : index * STEP + WIRE]

    for head in range(0, heads_here, 2):
        pair = (head, head + 1)
        for turn, found in zip(pair, projected(*[apart(turn) for turn in pair], tokens)):
            own = pl.ds(turn * HD, HD)
            q_ref[:, own] = rotated(found, gain_ref[0, 0:1, own], tokens)
        weights = [apart(heads_here + turn) for turn in pair]
        for turn, found in zip(pair, projected(*weights, 2 * tokens)):
            own = pl.ds(turn * HD, HD)
            k_ref[:, own] = rotated(found, gain_ref[1, 0:1, own], 2 * tokens).astype(BF16)
        weights = [rows[heads_here + 2 * turn + 1, 0:WIRE] for turn in pair]
        for turn, found in zip(pair, projected(*weights, 2 * tokens)):
            v_ref[:, pl.ds(turn * HD, HD)] = (found * inverse).astype(BF16)


def heads_rows(counts, left, mine, theirs, spread, cosine, sine, gains, heads_here):
    both = left.shape[0]
    wide = heads_here * HD
    return pl.pallas_call(
        functools.partial(heads_kernel, heads_here),
        out_shape=[
            jax.ShapeDtypeStruct((both // 2, wide), F32),
            jax.ShapeDtypeStruct((both, wide), BF16),
            jax.ShapeDtypeStruct((both, wide), BF16),
        ],
        in_specs=[smem()] + [vmem()] * 7,
        out_specs=[vmem()] * 3,
        scratch_shapes=[pltpu.VMEM((3 * heads_here, STEP, HD), BF16)],
        compiler_params=params(),
        name="heads_rows",
    )(counts, left, mine, theirs, spread, cosine, sine, gains)


def attend_kernel(
    heads_here, counts_ref, q_ref, k_ref, v_ref, left_ref, turned_ref, theirs_ref, *refs
):
    gram_refs, (out_ref, found, sems) = refs[:-3], refs[-3:]
    tokens = q_ref.shape[0]
    place = lax.axis_index("seq")
    count_own, count_other = counts_ref[place], counts_ref[jnp.bitwise_xor(place, 1)]

    left = left_ref[0:tokens, 0:WIRE]
    turned = turned_ref[0:WIRE]
    last = theirs_ref.shape[2] - HD
    gram = sum(ref[...].astype(F32) for ref in gram_refs)
    for place in range(2):
        gram = gram + theirs_ref[place, :, last:].astype(F32)
    gram = gram * (1.0 / D)
    gram_q, gram_k = [exact_pieces(values, 2) for values in gram_halves(gram)]
    spun_q = sum(jnp.dot(left, piece, preferred_element_type=F32) for piece in gram_q)
    wide_left = left_ref[0:tokens].astype(F32)
    square_q = jnp.sum(spun_q * wide_left[:, 0:WIRE], axis=1, keepdims=True)
    spread_q = wide_left[:, 65:66] + wide_left[:, 68:69]
    scale_q = lax.rsqrt(square_q + EPSILON * spread_q * spread_q) * (
        math.log2(math.e) / math.sqrt(HD)
    )
    scale_q = jnp.broadcast_to(scale_q, (tokens, HD))
    spun_k = sum(jnp.dot(piece, turned, preferred_element_type=F32) for piece in gram_k)
    wide_turned = turned.astype(F32)
    square_k = jnp.sum(spun_k * wide_turned, axis=0, keepdims=True)
    spread_k = wide_turned[65:66] + wide_turned[68:69]
    scale_k = lax.rsqrt(square_k + EPSILON * spread_k * spread_k)
    slot = lax.broadcasted_iota(jnp.int32, (1, 2 * tokens), 1)
    valid = slot < jnp.where(slot < tokens, count_own, tokens + count_other)
    scale_k = jnp.where(valid, scale_k, 0.0)

    slot = lax.broadcasted_iota(jnp.int32, (2 * tokens, HD), 0)
    valid = slot < jnp.where(slot < tokens, count_own, tokens + count_other)
    ones = jnp.where(valid, 1.0, 0.0).astype(BF16)
    row = lax.broadcasted_iota(jnp.int32, (tokens, HD), 0)
    contract = (((1,), (1,)), ((), ()))

    def scores_of(head):
        own = pl.ds(head * HD, HD)
        query = (q_ref[:, own] * scale_q).astype(BF16)
        return lax.dot_general(query, k_ref[:, own], contract, preferred_element_type=F32)

    copies = []
    scores = scores_of(0)
    for head in range(heads_here):
        own = pl.ds(head * HD, HD)
        later = scores_of(head + 1) if head + 1 < heads_here else None
        weights = jnp.exp2(scores * scale_k).astype(BF16)
        values = jnp.concatenate([v_ref[:, own], ones], axis=1)
        result = jnp.dot(weights, values, preferred_element_type=F32)
        result = result[:, 0:HD] / result[:, HD:]
        found[:, own] = jnp.where(row < count_own, result, 0.0).astype(BF16)
        copies.append(pltpu.make_async_copy(found.at[:, own], out_ref.at[:, own], sems.at[head]))
        copies[-1].start()
        scores = later
    for copy in copies:
        copy.wait()


def attend_rows(counts, queries, keys, values, left, turned, theirs, grams):
    heads_here = queries.shape[1] // HD
    return pl.pallas_call(
        functools.partial(attend_kernel, heads_here),
        out_shape=jax.ShapeDtypeStruct(queries.shape, BF16),
        in_specs=[smem()] + [vmem()] * (6 + len(grams)),
        out_specs=pl.BlockSpec(memory_space=pl.ANY),
        scratch_shapes=[
            pltpu.VMEM(queries.shape, BF16),
            pltpu.SemaphoreType.DMA((heads_here,)),
        ],
        compiler_params=params(),
        name="attend_rows",
    )(counts, queries, keys, values, left, turned, theirs, *grams)


def shards(
    patches,
    clip_shape,
    shard_counts,
    patch_weight,
    patch_bias,
    time_mod,
    block_mod,
    w_query,
    query_bias,
    w_keyvalue,
    keyvalue_bias,
    norm_gain,
):
    tokens = patches.shape[0]
    heads_here = w_query.shape[1] // HD
    count = lax.axis_size("seq")
    halves = lax.axis_size("mp")
    place = lax.axis_index("seq")
    clips = time_mod.shape[0]
    rows = w_query.shape[0]
    padded = -(-rows // 16) * 16
    clips_sent = count // 4

    def pad_rows(values):
        return values if rows == padded else jnp.pad(values, ((0, padded - rows), (0, 0)))

    packed = pack_weights(pad_rows(w_query), pad_rows(w_keyvalue))
    pieces = [packed[0]] + [swap_bits(packed[flip], 2 * flip) for flip in range(1, BLOCKS)]
    first_swapped = swap_bits(packed[0], 1)

    features = patch_bias.shape[0]
    own, own_patches = prepare_rows(
        patch_weight, patch_bias[None], time_mod, block_mod, patches, first_swapped
    )
    other = lax.ppermute(own, "mp", [(i, (i + 1) % halves) for i in range(halves)])
    other_patches = swap_bits(own_patches, 1)
    span = 8 * rows

    def group_part(values):
        if span == features and rows == padded:
            return values
        values = lax.dynamic_slice_in_dim(values, place // 8 * span % features, span, 1)
        values = jnp.pad(
            values.reshape(-1, 8, rows), ((0, 0), (0, 0), (0, padded - rows))
        )
        return values.reshape(-1, 8 * padded)

    rows_here = modulated_rows(
        own, other, group_part(own), group_part(other), clips_sent, span
    )
    placed = {0: packed[0], 1: first_swapped}
    for flip in reversed(range(1, BLOCKS)):
        piece = after(pieces[flip], rows_here, other_patches)
        placed[2 * flip], placed[2 * flip + 1] = piece, swap_bits(piece, 1)
    first = {order: placed.pop(order) for order in (6, 4, 5, 2, 3, 0, 1)}
    early = early_rows(rows_here, first, padded)

    products = product_rows(rows_here, early, placed, clips_sent, padded)
    arrived = {}
    for flip in [0, *range(2, clips_sent - 1), 1, clips_sent - 1]:
        pairs = []
        for source in range(count):
            rest, second, core = source // 4, source // 2 % 2, source % 2
            turn = flip % 2
            pairs.append((source, (rest ^ flip) * 4 + (core ^ turn) * 2 + (second ^ turn)))
        arrived[flip] = lax.ppermute(products[flip], "seq", pairs)
    biases = (query_bias[None], keyvalue_bias[None])
    left, turned, spread, cosine, sine, gains, bias = spread_rows(
        clip_shape,
        shard_counts,
        own_patches,
        other_patches,
        own,
        other,
        norm_gain,
        biases,
        products[0],
    )

    mine, gram, gram_sent = sum_rows(arrived, bias, w_query.shape[1], w_keyvalue.shape[1], (left,))
    theirs = swap_bits(mine, 1)
    far_mp = [(i, (i + 1) % halves) for i in range(halves)]
    far_both = [
        (core * halves + i, (core ^ 1) * halves + j) for core in range(count) for i, j in far_mp
    ]
    grams = (
        gram,
        lax.ppermute(gram_sent, "mp", far_mp),
        lax.ppermute(gram_sent, ("seq", "mp"), far_both),
    )
    queries, keys, values = heads_rows(
        shard_counts, left, mine, theirs, spread, cosine, sine, gains, heads_here
    )
    return attend_rows(shard_counts, queries, keys, values, left, turned, theirs, grams)


def solution(mesh):
    return jax.shard_map(
        shards,
        mesh=mesh,
        in_specs=(
            P("seq", None),
            P(),
            P(),
            P(None, "mp"),
            P("mp"),
            P(None, None, "mp"),
            P(None, "mp"),
            P("seq", "mp"),
            P("mp"),
            P("seq", "mp"),
            P("mp"),
            P(None, "mp"),
        ),
        out_specs=P("seq", "mp"),
        check_vma=False,
    )
```
